256 devices in a mesh: cand: 8 (over x, core), ctx: 8 (over y, z_hi), mp: 4 (over z_lo).
Axes of the slice: x: 4, y: 4, z: 8 (z_hi: 2, z_lo: 4; z = z_hi * 4 + z_lo), core: 2. Of those that a mesh axis runs over, the one named last changes fastest.
Arguments:
- states: bfloat16 [384, 4096], P('ctx'), may hold values from -6 to 6
- attn_gain: float32 [4096], replicated, may hold values from 0.25 to 1.75
- w_query: bfloat16 [4096, 8, 512], P('cand', 'mp'), may hold values from -0.25 to 0.25
- w_keyval: bfloat16 [4096, 8, 256], P('cand', 'mp'), may hold values from -0.09375 to 0.09375
- kv_cache: bfloat16 [6144, 8, 256], P('ctx', 'mp'), may hold values from -6 to 6
- page_live: int32 [48], P('ctx'), may hold values 0 or 1
- factor_levels: float32 [16], replicated, may hold values from 1 to 32
- cand_index: int32 [8, 64], P('cand'), may hold values from 0 to 15
- w_out: bfloat16 [4096, 4096], P(None, ('cand', 'mp')), may hold values from -0.09375 to 0.09375
- ffn_gain: float32 [4096], replicated, may hold values from 0.25 to 1.75
- w_gate_up: bfloat16 [2, 4096, 14336], P(None, 'ctx', ('cand', 'mp')), may hold values from -0.09375 to 0.09375
- w_down: bfloat16 [14336, 4096], P(('cand', 'mp')), may hold values from -0.09375 to 0.09375
Outputs:
- layer_out: bfloat16 [8, 384, 4096], P(None, 'ctx', ('cand', 'mp'))
The draws below stay inside these ranges and needn't reach their ends.
All inputs are finite; a program needn't handle non-finite values. No bound on the sum of `page_live` on one device may be relied on, other than what follows from the above.
Results may differ from the reference program's by a relative error of at most 0.02.
Values may be sent and summed in bfloat16 or wider, within the bound.
A program may use at most 64 MiB of HBM per device.

```python
import math
import jax
import jax.numpy as jnp
from jax import lax

D = 4096
H = 32
KVH = 8
HD = 128
FF = 14336
PAGE = 128
LEVELS = 16
GQ = 4
QUERIES = 384
CACHE = 6144
PAGES = 48
CANDS = 8


def plant(result, key, smallest, largest):
    longest = result.shape.index(max(result.shape))
    spots = []
    for shift in (0, 1):
        where = [jax.random.randint(jax.random.fold_in(key, axis), (), 0, length) for axis, length in enumerate(result.shape)]
        where[longest] = (where[longest] + shift) % result.shape[longest]
        spots.append(tuple(where))
    return result.at[spots[0]].set(smallest).at[spots[1]].set(largest)


def raised(drawn, own_key, source, target, shards_of, factor):
    def block_of(dim):
        return (jnp.arange(drawn.shape[dim]) // (drawn.shape[dim] // shards_of)).reshape((-1,) + (1,) * (drawn.ndim - 1 - dim))

    first = jax.random.permutation(own_key, shards_of)[block_of(target)]
    other_side = (block_of(target) + shards_of // 2) % shards_of
    return jnp.where((block_of(source) == first) | (block_of(source) == other_side), factor * drawn, drawn)


def steps_of(stream_key, shape, shards, low, top_value):
    level = 1.0
    for axis_at, shards_of in shards:
        draws = jax.random.uniform(jax.random.fold_in(jax.random.fold_in(stream_key, 6), axis_at), (shards_of,), jnp.float32, low / len(shards), top_value / len(shards))
        level = level * jnp.repeat(jnp.exp(draws), shape[axis_at] // shards_of).reshape((-1,) + (1,) * (len(shape) - 1 - axis_at))
    return level


def normal_values(stream_key, extent, deviation, bound, pieces=(), kind=jnp.bfloat16):
    result = deviation * jax.random.normal(stream_key, extent, jnp.float32)
    if pieces:
        result = result * steps_of(stream_key, extent, pieces, -0.22, 0.18)
    return jnp.clip(result, -bound, bound).astype(kind)


def noise_with(stream_key, shape, deviation, limit, cuts, heavy, kind=jnp.bfloat16):
    drawn = deviation * jax.random.normal(stream_key, shape, jnp.float32)
    if cuts:
        drawn = drawn * steps_of(stream_key, shape, cuts, -0.22, 0.18)
    return jnp.clip(raised(drawn, jax.random.fold_in(stream_key, 3), *heavy), -limit, limit).astype(kind)


def setup_inputs(seed: int = 0) -> dict:
    seeds = jax.random.split(jax.random.key(seed), 13)
    states = normal_values(seeds[0], (QUERIES, D), 1.0, 6.0, ((0, 8),))
    attn_gain = jnp.clip(1.0 + 0.15 * jax.random.normal(seeds[1], (D,), jnp.float32), 0.25, 1.75)
    w_query = normal_values(seeds[2], (D, KVH, GQ * HD), (D // 9) ** -0.5, 0.25, ((0, 8), (1, 4)))
    w_keyval = normal_values(seeds[3], (D, KVH, 2 * HD), D ** -0.5, 0.09375, ((0, 8), (1, 4)))
    kv_cache = normal_values(seeds[4], (CACHE, KVH, 2 * HD), 1.0, 6.0, ((0, 8), (1, 4)))
    page_live = plant((jax.random.randint(seeds[5], (PAGES,), 0, 4) < 3).astype(jnp.int32), jax.random.fold_in(seeds[5], 1), 0, 1)
    factor_levels = jnp.clip(jnp.exp(jax.random.uniform(seeds[6], (LEVELS,), jnp.float32, math.log(1.0), math.log(32.0))), 1.0, 32.0)
    cand_index = plant(jax.random.randint(seeds[7], (CANDS, HD // 2), 0, LEVELS), jax.random.fold_in(seeds[7], 1), 0, LEVELS - 1).astype(jnp.int32)
    w_out = normal_values(seeds[8], (H * HD, D), (H * HD) ** -0.5, 0.09375, ((1, 32),))
    ffn_gain = jnp.clip(1.0 + 0.15 * jax.random.normal(seeds[9], (D,), jnp.float32), 0.25, 1.75)
    w_gate_up = normal_values(seeds[10], (2, D, FF), D ** -0.5, 0.09375, ((1, 8), (2, 32)))
    w_down = noise_with(seeds[11], (FF, D), FF ** -0.5, 0.09375, ((0, 32),), (0, 1, 32, 2.75))
    return {"states": states, "attn_gain": attn_gain, "w_query": w_query, "w_keyval": w_keyval, "kv_cache": kv_cache, "page_live": page_live, "factor_levels": factor_levels, "cand_index": cand_index, "w_out": w_out, "ffn_gain": ffn_gain, "w_gate_up": w_gate_up, "w_down": w_down}


EPSILON = 1e-05
ROPE_BASE = 500000.0

def rms_scale(values, gain):
    return values * lax.rsqrt(lax.optimization_barrier(jnp.mean(values * values, axis=-1, keepdims=True)) + EPSILON) * gain

def base_freq(half):
    steps = jnp.arange(half, dtype=jnp.float32)
    return jnp.exp(steps * (-2.0 * math.log(ROPE_BASE) / (2 * half)))

def rotate(values, position, freq):
    half = freq.shape[0]
    angle = position[:, None] * freq[None, :]
    cosine = jnp.cos(angle)[:, None, :]
    sine = jnp.sin(angle)[:, None, :]
    first = values[..., :half]
    second = values[..., half:]
    return jnp.concatenate([first * cosine - second * sine, second * cosine + first * sine], axis=-1)

def reference(states, attn_gain, w_query, w_keyval, kv_cache, page_live, factor_levels, cand_index, w_out, ffn_gain, w_gate_up, w_down):
    f32 = jnp.float32
    bf16 = jnp.bfloat16
    normed = rms_scale(states.astype(f32), attn_gain).astype(bf16)
    query = jnp.dot(normed, w_query.reshape(D, KVH * GQ * HD), preferred_element_type=f32).astype(bf16)
    query = query.reshape(QUERIES, H, HD)
    keyval = jnp.dot(normed, w_keyval.reshape(D, KVH * 2 * HD), preferred_element_type=f32).astype(bf16)
    keyval = keyval.reshape(QUERIES, KVH, 2 * HD)
    half = HD // 2
    picks = (cand_index[:, :, None] == jnp.arange(LEVELS, dtype=jnp.int32)[None, None, :]).astype(f32)
    factors = lax.optimization_barrier(jnp.sum(picks * factor_levels[None, None, :], axis=-1))
    freqs = base_freq(half)[None, :] / factors
    query_pos = (CACHE + jnp.arange(QUERIES, dtype=jnp.int32)).astype(f32)
    cache_pos = jnp.arange(CACHE, dtype=jnp.int32).astype(f32)
    live = jnp.repeat(page_live, PAGE) == 1
    causal = jnp.arange(QUERIES, dtype=jnp.int32)[None, :] <= jnp.arange(QUERIES, dtype=jnp.int32)[:, None]
    key_live = jnp.concatenate([jnp.broadcast_to(live[None, :], (QUERIES, CACHE)), causal], axis=1)
    values_all = jnp.concatenate([kv_cache[..., HD:], keyval[..., HD:]], axis=0)
    scale = HD ** (-0.5)

    def one_candidate(freq):
        query_rot = rotate(query.astype(f32), query_pos, freq).astype(bf16).reshape(QUERIES, KVH, GQ, HD)
        cache_keys = rotate(kv_cache[..., :HD].astype(f32), cache_pos, freq)
        recent_keys = rotate(keyval[..., :HD].astype(f32), query_pos, freq)
        keys = jnp.concatenate([cache_keys, recent_keys], axis=0).astype(bf16)
        query_rot = lax.optimization_barrier(query_rot)
        keys = lax.optimization_barrier(keys)

        def one_head(operands):
            head_query, head_keys, head_values = operands
            scores = jnp.einsum('tgd,nd->tgn', head_query.astype(f32), head_keys.astype(f32)) * scale
            expo = jnp.where(key_live[:, None, :], jnp.exp(scores), 0.0)
            denom = lax.optimization_barrier(jnp.sum(expo, axis=-1))
            weights = lax.optimization_barrier(expo.astype(bf16)).astype(f32)
            summed = jnp.einsum('tgn,nd->tgd', weights, head_values.astype(f32))
            return (summed / denom[..., None]).astype(bf16)
        heads_out = lax.map(one_head, (jnp.transpose(query_rot, (1, 0, 2, 3)), jnp.transpose(keys, (1, 0, 2)), jnp.transpose(values_all, (1, 0, 2))))
        attn = jnp.transpose(heads_out, (1, 0, 2, 3)).reshape(QUERIES, H * HD)
        resid = states.astype(f32) + jnp.dot(attn, w_out, preferred_element_type=f32)
        ffn_in = rms_scale(resid, ffn_gain).astype(bf16)
        gate = jnp.dot(ffn_in, w_gate_up[0], preferred_element_type=f32)
        upward = jnp.dot(ffn_in, w_gate_up[1], preferred_element_type=f32)
        inner = (jax.nn.silu(gate) * upward).astype(bf16)
        return (resid + jnp.dot(inner, w_down, preferred_element_type=f32)).astype(bf16)
    return lax.map(one_candidate, freqs)
```

```python
import functools
import math

import jax
import jax.numpy as jnp
from jax import lax
from jax.experimental import pallas as pl
from jax.experimental.pallas import tpu as pltpu
from jax.sharding import PartitionSpec as P

EPSILON = 1e-05
ROPE_BASE = 500000.0
MESH = pl.DeviceIdType.MESH
F32 = jnp.float32
BF16 = jnp.bfloat16
DMA = pltpu.SemaphoreType.DMA
VM = pltpu.VMEM


def position():
    c = lax.axis_index("cand")
    s = lax.axis_index("ctx")
    m = lax.axis_index("mp")
    return c // 2, c % 2, s // 2, s % 2, m


def dev(x, k, y, h, m):
    return {"cand": x * 2 + k, "ctx": y * 2 + h, "mp": m}


def up(value, step, size=4):
    return lax.rem(value + step, size)


def remote(src, dst, send_sem, recv_sem, target):
    return pltpu.make_async_remote_copy(
        src_ref=src,
        dst_ref=dst,
        send_sem=send_sem,
        recv_sem=recv_sem,
        device_id=target,
        device_id_type=MESH,
    )


def greet(peers):
    barrier = pltpu.get_barrier_semaphore()
    for peer in peers:
        pl.semaphore_signal(barrier, inc=1, device_id=peer, device_id_type=MESH)
    pl.semaphore_wait(barrier, len(peers))


def turn(values, cosine, sine):
    return values * cosine + pltpu.roll(values, 64, 1) * sine


def attend_kernel(
    part,
    key_cos,
    key_sin,
    new_cos,
    new_sin,
    kv,
    flags,
    w_shard,
    attn,
    w_all,
    rs_in,
    q_own,
    n_own,
    q_all,
    n_all,
    kv_far,
    flags_far,
    keys,
    vals,
    new_keys,
    new_vals,
    live,
    q_rot,
    num_out,
    num_in,
    num_own,
    den_out,
    den_in,
    den_own,
    rs_s,
    rs_r,
    q_s,
    q_r,
    n_s,
    n_r,
    kz_s,
    kz_r,
    kf_s,
    kf_r,
    fl_s,
    fl_r,
    w_s,
    w_r,
    num_s,
    num_r,
    den_s,
    den_r,
    loc,
):
    x, k, y, h, m = position()
    c = x * 2 + k
    far = 1 - h
    cand_peers = [(x, 1 - k)] + [(up(x, i), kk) for i in (1, 2, 3) for kk in (k, 1 - k)]
    xy_peers = [(up(x, i), up(y, j)) for j in range(4) for i in range(4) if i or j]
    zhi = dev(x, k, y, far, m)
    greet(
        [dev(a, b, y, h, m) for a, b in cand_peers]
        + [dev(a, k, b, h, m) for a, b in xy_peers[3:]]
        + [dev(up(x, i), k, y, far, m) for i in range(4)]
    )
    rows = kv_far.shape[1]
    sends = []

    def go(copy):
        copy.start()
        sends.append(copy)
        return copy

    for i, (a, b) in enumerate(cand_peers):
        go(remote(part.at[a], rs_in.at[i], rs_s.at[i], rs_r.at[i], dev(a, b, y, h, m)))
    mine = kv.at[pl.ds(pl.multiple_of(c * rows, 16), rows)]
    kz = go(remote(mine, kv_far.at[c], kz_s, kz_r, zhi))
    fl = go(remote(flags, flags_far, fl_s, fl_r, zhi))
    w_local = pltpu.make_async_copy(w_shard, w_all.at[y], loc)
    w_local.start()
    w_copies = []
    for i in (1, 2, 3):
        w_copies.append(
            go(remote(w_shard, w_all.at[y], w_s.at[i], w_r.at[i], dev(x, k, up(y, i), h, m)))
        )
    w_copies.append(go(remote(w_shard, w_all.at[4], w_s.at[0], w_r.at[0], zhi)))

    half = kv.shape[0]

    def place(block, where, source):
        for j in range(2):
            raw = source[:, j * 256 : j * 256 + 128].astype(F32)
            keys[j, where, :] = turn(raw, block[0], block[1]).astype(BF16)
            vals[j, where, :] = source[:, j * 256 + 128 : j * 256 + 256]

    place((key_cos[0], key_sin[0]), pl.ds(0, half), kv[...])
    for j in range(2):
        new_keys[j] = jnp.zeros(new_keys.shape[1:], BF16)
        new_vals[j] = jnp.zeros(new_vals.shape[1:], BF16)

    for i, (a, b) in enumerate(cand_peers):
        remote(part.at[a], rs_in.at[i], rs_s.at[i], rs_r.at[i], dev(a, b, y, h, m)).wait_recv()
    total = part[x].astype(F32)
    for i in range(7):
        total = total + rs_in[i].astype(F32)
    summed = total.astype(BF16)
    q_own[...] = summed[:, :256]
    n_own[...] = summed[:, 256:]
    q_all[y, x] = summed[:, :256]
    n_all[0, x] = summed[:, 256:]
    for i, (a, b) in enumerate(xy_peers):
        go(remote(q_own, q_all.at[y, x], q_s.at[i], q_r.at[i], dev(a, k, b, h, m)))
    for i in (1, 2, 3):
        go(remote(n_own, n_all.at[0, x], n_s.at[i], n_r.at[i], dev(up(x, i), k, y, h, m)))
    for i in range(4):
        go(remote(n_own, n_all.at[1, x], n_s.at[4 + i], n_r.at[4 + i], dev(up(x, i), k, y, far, m)))

    kz.wait_recv()
    for i, (a, b) in enumerate(cand_peers):
        go(remote(kv_far.at[c], kv_far.at[c], kf_s.at[i], kf_r.at[i], dev(a, b, y, h, m)))
    fl.wait_recv()
    for page in range(6):
        live[:, page * 128 : page * 128 + 128] = jnp.broadcast_to(flags[:, page : page + 1], (8, 128))
        live[:, half + page * 128 : half + page * 128 + 128] = jnp.broadcast_to(
            flags_far[:, page : page + 1], (8, 128)
        )

    for i, (a, b) in enumerate(xy_peers):
        remote(q_own, q_all.at[b, a], q_s.at[i], q_r.at[i], dev(a, k, b, h, m)).wait_recv()

    def turn_queries(b, carry):
        cosine = new_cos[2 * b + h]
        sine = new_sin[2 * b + h]
        for head in range(8):
            raw = q_all[b, head // 2, :, (head % 2) * 128 : (head % 2) * 128 + 128].astype(F32)
            spot = (head % 4) * 48
            q_rot[head // 4, b, spot : spot + 48, :] = turn(raw, cosine, sine).astype(BF16)
        return carry

    lax.fori_loop(0, 4, turn_queries, 0)

    for i in (1, 2, 3):
        remote(n_own, n_all.at[0, x], n_s.at[i], n_r.at[i], zhi).wait_recv()
    for i in range(4):
        remote(n_own, n_all.at[1, x], n_s.at[4 + i], n_r.at[4 + i], zhi).wait_recv()
    for block in range(2):
        owner = 2 * y + (h if block == 0 else far)
        for j in range(2):
            raw = n_all[block, 2 * j].astype(F32)
            spot = block * 48
            new_keys[j, spot : spot + 48, :] = turn(raw, new_cos[owner], new_sin[owner]).astype(BF16)
            new_vals[j, spot : spot + 48, :] = n_all[block, 2 * j + 1]

    for i, (a, b) in enumerate(cand_peers):
        remote(
            kv_far.at[c], kv_far.at[a * 2 + b], kf_s.at[i], kf_r.at[i], dev(a, b, y, h, m)
        ).wait_recv()
    place(
        (key_cos[1], key_sin[1]),
        pl.ds(half, half),
        kv_far[...].reshape(half, kv.shape[1]),
    )

    scale = 128 ** (-0.5)
    lane = lax.broadcasted_iota(jnp.int32, (48, 128), 1)
    key_lane = lax.broadcasted_iota(jnp.int32, (192, 128), 1)
    token = lax.broadcasted_iota(jnp.int32, (4, 48, 128), 1).reshape(192, 128)
    first = (2 * y + h) * 48
    second = (2 * y + far) * 48
    key_index = jnp.where(
        key_lane < 48, first + key_lane, jnp.where(key_lane < 96, second + key_lane - 48, 1 << 20)
    )
    nt = (((1,), (1,)), ((), ()))

    def attend(step, carry):
        j = step // 4
        i = step % 4
        b = up(y, i + 1)
        query = q_rot[j, b]
        scores = lax.dot_general(query, keys[j], nt, preferred_element_type=F32)
        expo = jnp.where(live[0:1, :] > 0.5, jnp.exp(scores * scale), 0.0)
        recent = lax.dot_general(query, new_keys[j], nt, preferred_element_type=F32)
        seen = key_index <= (2 * b + h) * 48 + token
        recent_expo = jnp.where(seen, jnp.exp(recent * scale), 0.0)
        denom = jnp.sum(expo, axis=1, keepdims=True) + jnp.sum(recent_expo, axis=1, keepdims=True)
        numer = jnp.dot(expo.astype(BF16), vals[j], preferred_element_type=F32)
        numer = numer + jnp.dot(recent_expo.astype(BF16), new_vals[j], preferred_element_type=F32)
        lanes = jnp.zeros((48, 128), F32)
        for g in range(4):
            lanes = lanes + jnp.where(lane == j * 4 + g, denom[g * 48 : g * 48 + 48], 0.0)

        @pl.when(i < 3)
        def _():
            num_out[j, i] = numer.astype(BF16)
            remote(
                num_out.at[j, i], num_in.at[j, i], num_s.at[j, i], num_r.at[j, i], dev(x, k, b, h, m)
            ).start()

            @pl.when(j == 0)
            def _():
                den_out[i] = lanes

            @pl.when(j == 1)
            def _():
                den_out[i] = den_out[i] + lanes
                remote(
                    den_out.at[i], den_in.at[i], den_s.at[i], den_r.at[i], dev(x, k, b, h, m)
                ).start()

        @pl.when(i == 3)
        def _():
            num_own[j] = numer

            @pl.when(j == 0)
            def _():
                den_own[...] = lanes

            @pl.when(j == 1)
            def _():
                den_own[...] = den_own[...] + lanes

        return carry

    lax.fori_loop(0, 8, attend, 0)

    denom = den_own[...]
    for i in range(3):
        copy = remote(den_out.at[i], den_in.at[i], den_s.at[i], den_r.at[i], dev(x, k, up(y, i + 1), h, m))
        copy.wait()
        denom = denom + den_in[i]
    for j in range(2):
        numer = num_own[j]
        for i in range(3):
            remote(
                num_out.at[j, i],
                num_in.at[j, i],
                num_s.at[j, i],
                num_r.at[j, i],
                dev(x, k, up(y, i + 1), h, m),
            ).wait()
            numer = numer + num_in[j, i].astype(F32)
        for g in range(4):
            head = j * 4 + g
            attn[:, head * 128 : head * 128 + 128] = (
                numer[g * 48 : g * 48 + 48] / denom[:, head : head + 1]
            ).astype(BF16)

    w_local.wait()
    for copy in w_copies:
        copy.wait_recv()
    for copy in sends:
        copy.wait_send()


def feed_kernel(
    attn,
    states,
    gain,
    w_out,
    w_all,
    w_down,
    out,
    attn_all,
    out_w,
    gate_up_w,
    down_w,
    resid,
    shard,
    shards,
    normed,
    acc,
    inner,
    x_out,
    x_in,
    x_own,
    z_out,
    z_in,
    swap_out,
    swap_in,
    loc,
    core_s,
    core_r,
    y_s,
    y_r,
    cy_s,
    cy_r,
    az_s,
    az_r,
    ax_s,
    ax_r,
    gz_s,
    gz_r,
    gx_s,
    gx_r,
    rx_s,
    rx_r,
    rz_s,
    rz_r,
    sw_s,
    sw_r,
):
    x, k, y, h, m = position()
    far = 1 - h
    x_peers = [up(x, i) for i in (1, 2, 3)]
    y_peers = [up(y, i) for i in (1, 2, 3)]
    m_peers = [up(m, i) for i in (1, 2, 3)]
    twin = dev(x, 1 - k, y, h, m)

    def at_x(a):
        return dev(a, k, y, h, m)

    def at_m(a):
        return dev(x, k, y, h, a)

    greet(
        [twin]
        + [at_x(a) for a in x_peers]
        + [dev(x, k, a, h, m) for a in y_peers]
        + [at_m(a) for a in m_peers]
    )
    sends = []

    def go(copy):
        copy.start()
        sends.append(copy)
        return copy

    def gather(view, zs, zr, xs, xr):
        own = view(x, m)
        for i, b in enumerate(m_peers):
            go(remote(own, own, zs.at[i], zr.at[i], at_m(b)))
        for j, a in enumerate(x_peers):
            go(remote(own, own, xs.at[3, j], xr.at[3, j], at_x(a)))
        for i in range(3):
            came = view(x, up(m, 3 - i))
            remote(own, came, zs.at[i], zr.at[i], at_m(m_peers[i])).wait_recv()
            for j, a in enumerate(x_peers):
                go(remote(came, came, xs.at[i, j], xr.at[i, j], at_x(a)))

    def gather_rest(view, xs, xr):
        for i in (3, 0, 1, 2):
            for j in range(3):
                came = view(up(x, 3 - j), up(m, 3 - i) if i < 3 else m)
                remote(came, came, xs.at[i, j], xr.at[i, j], at_x(x_peers[j])).wait_recv()

    def attn_view(a, b):
        return attn_all.at[b, pl.ds(pl.multiple_of(a * 48, 16), 48)]

    attn_all[m, pl.ds(pl.multiple_of(x * 48, 16), 48), :] = attn[...]
    w_far = 2 * y + far
    y_copies = [
        go(
            remote(
                w_all.at[4], gate_up_w.at[k, w_far], y_s.at[i], y_r.at[i], dev(x, k, b, h, m)
            )
        )
        for i, b in enumerate(y_peers)
    ]
    side = pl.ds(pl.multiple_of(k * 128, 128), 128)
    pairs = [(w_out, out_w.at[:, side])]
    pairs += [(w_all.at[b], gate_up_w.at[k, 2 * b + h]) for b in range(4)]
    pairs += [(w_all.at[4], gate_up_w.at[k, w_far]), (w_down, down_w.at[k])]
    local = []
    shared = []
    for i, (src, dst) in enumerate(pairs):
        copy = pltpu.make_async_copy(src, dst, loc.at[i])
        copy.start()
        local.append(copy)
        shared.append(go(remote(src, dst, core_s.at[i], core_r.at[i], twin)))

    gather(attn_view, az_s, az_r, ax_s, ax_r)
    gather_rest(attn_view, ax_s, ax_r)
    local[0].wait()
    shared[0].wait_recv()

    total = jnp.dot(attn_all[0], out_w[0:1024, :], preferred_element_type=F32)
    for b in range(1, 4):
        total = total + jnp.dot(
            attn_all[b], out_w[b * 1024 : b * 1024 + 1024, :], preferred_element_type=F32
        )
    even = pl.ds(pl.multiple_of((8 * x + m) * 128, 128), 128)
    odd = pl.ds(pl.multiple_of((8 * x + 4 + m) * 128, 128), 128)
    columns = jnp.concatenate([states[:, even], states[:, odd]], axis=1).astype(F32)
    gains = jnp.concatenate([gain[:, even], gain[:, odd]], axis=1)
    kept = total + jnp.concatenate([columns] * 4, axis=0)
    resid[...] = kept

    def shard_view(a, b):
        return shards.at[a, b]

    shards[x, m] = (kept * gains).astype(BF16)
    gather(shard_view, gz_s, gz_r, gx_s, gx_r)

    passed = []
    for i in range(3):
        came = gate_up_w.at[k, 2 * up(y, 3 - i) + far]
        remote(w_all.at[4], came, y_s.at[i], y_r.at[i], twin).wait_recv()
        passed.append(go(remote(came, came, cy_s.at[i], cy_r.at[i], twin)))
    gather_rest(shard_view, gx_s, gx_r)

    squares = jnp.zeros((192, 128), F32)
    for a in range(4):
        for b in range(4):
            for e in range(2):
                block = shards[a, b, :, e * 128 : e * 128 + 128]
                normed[2 * a + e, :, b * 128 : b * 128 + 128] = block
                spot = (8 * a + 4 * e + b) * 128
                plain = block.astype(F32) / gain[:, spot : spot + 128]
                squares = squares + plain * plain
    ratio = lax.rsqrt(jnp.sum(squares, axis=1, keepdims=True) / 4096 + EPSILON)

    for copy in local[1:]:
        copy.wait()
    for copy in shared[1:]:
        copy.wait_recv()
    for copy in passed:
        copy.wait_recv()

    acc[...] = jnp.zeros(acc.shape, F32)
    nt = (((1,), (1,)), ((), ()))

    def gate_up(s, carry):
        for cc in range(2):
            for part in range(2):
                acc[cc, part] = acc[cc, part] + lax.dot_general(
                    normed[s],
                    gate_up_w[cc, s, part * 448 : part * 448 + 448, :],
                    nt,
                    preferred_element_type=F32,
                )
        return carry

    lax.fori_loop(0, 8, gate_up, 0)
    for cc in range(2):
        gate = acc[cc, 0] * ratio
        upward = acc[cc, 1] * ratio
        inner[cc] = (gate / (1.0 + jnp.exp(-gate)) * upward).astype(BF16)

    def down(step, carry):
        zi = step // 4
        xi = step % 4
        b = up(m, zi + 1)
        a = up(x, xi + 1)
        first = pl.ds(pl.multiple_of((8 * a + b) * 128, 128), 128)
        second = pl.ds(pl.multiple_of((8 * a + 4 + b) * 128, 128), 128)
        block = jnp.zeros((192, 256), F32)
        for cc in range(2):
            weights = jnp.concatenate([down_w[cc, :, first], down_w[cc, :, second]], axis=1)
            block = block + jnp.dot(inner[cc], weights, preferred_element_type=F32)

        @pl.when(xi < 3)
        def _():
            x_out[xi, zi] = block.astype(BF16)
            remote(
                x_out.at[xi, zi], x_in.at[xi, zi], rx_s.at[xi, zi], rx_r.at[xi, zi], at_x(a)
            ).start()

        @pl.when(xi == 3)
        def _():
            x_own[zi] = block

        return carry

    lax.fori_loop(0, 16, down, 0)
    for zi in range(4):
        block = x_own[zi]
        for xi in range(3):
            remote(
                x_out.at[xi, zi], x_in.at[xi, zi], rx_s.at[xi, zi], rx_r.at[xi, zi], at_x(x_peers[xi])
            ).wait()
            block = block + x_in[xi, zi].astype(F32)
        if zi < 3:
            z_out[zi] = block.astype(BF16)
            go(remote(z_out.at[zi], z_in.at[zi], rz_s.at[zi], rz_r.at[zi], at_m(m_peers[zi])))
    block = block + resid[...]
    for zi in range(3):
        remote(z_out.at[zi], z_in.at[zi], rz_s.at[zi], rz_r.at[zi], at_m(m_peers[zi])).wait_recv()
        block = block + z_in[zi].astype(F32)
    result = block.astype(BF16)
    lower = result[:, :128]
    upper = result[:, 128:]
    swap_out[...] = jnp.where(k == 0, upper, lower)
    swap = go(remote(swap_out, swap_in, sw_s, sw_r, twin))
    kept_half = jnp.where(k == 0, lower, upper)
    for a in range(4):
        out[a, k] = kept_half[a * 48 : a * 48 + 48]
    swap.wait_recv()
    for a in range(4):
        out[a, 1 - k] = swap_in[a * 48 : a * 48 + 48, :]
    for copy in sends:
        copy.wait_send()


def rms_scale(values, gain):
    return values * lax.rsqrt(jnp.mean(values * values, axis=-1, keepdims=True) + EPSILON) * gain


def base_freq(half):
    steps = jnp.arange(half, dtype=F32)
    return jnp.exp(steps * (-2.0 * math.log(ROPE_BASE) / (2 * half)))


def tables(where, freq):
    angle = where.astype(F32)[:, None] * freq[None, :]
    cosine = jnp.cos(angle)
    sine = jnp.sin(angle)
    return jnp.concatenate([cosine, cosine], axis=1), jnp.concatenate([-sine, sine], axis=1)


def per_device(
    states,
    attn_gain,
    w_query,
    w_keyval,
    kv_cache,
    page_live,
    factor_levels,
    cand_index,
    w_out,
    ffn_gain,
    w_gate_up,
    w_down,
):
    x, k, y, h, m = position()
    c = lax.axis_index("cand")
    normed = rms_scale(states.astype(F32), attn_gain).astype(BF16)
    slab = lax.dynamic_slice_in_dim(normed, c * 512, 512, 1)
    query_part = jnp.einsum("td,dkc->tkc", slab, w_query, preferred_element_type=F32)
    keyval_part = jnp.einsum("td,dkc->tkc", slab, w_keyval, preferred_element_type=F32)
    part = jnp.concatenate(
        [query_part.reshape(48, 4, 256), keyval_part.reshape(48, 4, 128)], axis=2
    ).astype(BF16)
    part = jnp.transpose(part, (1, 0, 2))
    picks = (cand_index[0][:, None] == jnp.arange(16, dtype=jnp.int32)[None, :]).astype(F32)
    factors = jnp.sum(picks * factor_levels[None, :], axis=-1)
    freq = base_freq(64) / factors
    spots = jnp.arange(768, dtype=jnp.int32)
    near = (2 * y + h) * 768 + spots
    far = (2 * y + 1 - h) * 768 + spots
    key_cos, key_sin = tables(jnp.concatenate([near, far]), freq)
    new_cos, new_sin = tables(6144 + jnp.arange(384, dtype=jnp.int32), freq)
    flags = jnp.pad((page_live == 1).astype(F32), (0, 122))
    flags = jnp.broadcast_to(flags[None, :], (8, 128))
    w_shard = jnp.swapaxes(w_gate_up, 1, 2).reshape(896, 512)

    vmem = pl.BlockSpec(memory_space=pltpu.VMEM)
    hbm = pl.BlockSpec(memory_space=pl.ANY)
    attn, w_all = pl.pallas_call(
        attend_kernel,
        out_shape=(
            jax.ShapeDtypeStruct((48, 1024), BF16),
            jax.ShapeDtypeStruct((5, 896, 512), BF16),
        ),
        in_specs=[vmem] * 7 + [hbm],
        out_specs=(vmem, hbm),
        scratch_shapes=[
            VM((7, 48, 384), BF16),
            VM((48, 256), BF16),
            VM((48, 128), BF16),
            VM((4, 4, 48, 256), BF16),
            VM((2, 4, 48, 128), BF16),
            VM((8, 96, 512), BF16),
            VM((8, 128), F32),
            VM((2, 1536, 128), BF16),
            VM((2, 1536, 128), BF16),
            VM((2, 128, 128), BF16),
            VM((2, 128, 128), BF16),
            VM((8, 1536), F32),
            VM((2, 4, 192, 128), BF16),
            VM((2, 3, 192, 128), BF16),
            VM((2, 3, 192, 128), BF16),
            VM((2, 192, 128), F32),
            VM((3, 48, 128), F32),
            VM((3, 48, 128), F32),
            VM((48, 128), F32),
            DMA((7,)),
            DMA((7,)),
            DMA((15,)),
            DMA((15,)),
            DMA((8,)),
            DMA((8,)),
            DMA,
            DMA,
            DMA((7,)),
            DMA((7,)),
            DMA,
            DMA,
            DMA((4,)),
            DMA((4,)),
            DMA((2, 3)),
            DMA((2, 3)),
            DMA((3,)),
            DMA((3,)),
            DMA,
        ],
        compiler_params=pltpu.CompilerParams(
            collective_id=0, has_side_effects=True, vmem_limit_bytes=32 << 20
        ),
        cost_estimate=pl.CostEstimate(
            flops=1400000000, bytes_accessed=8000000, transcendentals=2500000
        ),
        name="attend",
    )(
        part,
        key_cos.reshape(2, 768, 128),
        key_sin.reshape(2, 768, 128),
        new_cos.reshape(8, 48, 128),
        new_sin.reshape(8, 48, 128),
        kv_cache.reshape(768, 512),
        flags,
        w_shard,
    )

    out = pl.pallas_call(
        feed_kernel,
        out_shape=jax.ShapeDtypeStruct((4, 2, 48, 128), BF16),
        in_specs=[vmem] * 3 + [hbm] * 3,
        out_specs=vmem,
        scratch_shapes=[
            VM((4, 192, 1024), BF16),
            VM((4096, 256), BF16),
            VM((2, 8, 896, 512), BF16),
            VM((2, 448, 4096), BF16),
            VM((192, 256), F32),
            VM((192, 256), BF16),
            VM((4, 4, 192, 256), BF16),
            VM((8, 192, 512), BF16),
            VM((2, 2, 192, 448), F32),
            VM((2, 192, 448), BF16),
            VM((3, 4, 192, 256), BF16),
            VM((3, 4, 192, 256), BF16),
            VM((4, 192, 256), F32),
            VM((3, 192, 256), BF16),
            VM((3, 192, 256), BF16),
            VM((192, 128), BF16),
            VM((192, 128), BF16),
            DMA((7,)),
            DMA((7,)),
            DMA((7,)),
            DMA((3,)),
            DMA((3,)),
            DMA((3,)),
            DMA((3,)),
            DMA((3,)),
            DMA((3,)),
            DMA((4, 3)),
            DMA((4, 3)),
            DMA((3,)),
            DMA((3,)),
            DMA((4, 3)),
            DMA((4, 3)),
            DMA((3, 4)),
            DMA((3, 4)),
            DMA((3,)),
            DMA((3,)),
            DMA,
            DMA,
        ],
        compiler_params=pltpu.CompilerParams(
            collective_id=1, has_side_effects=True, vmem_limit_bytes=56 << 20
        ),
        cost_estimate=pl.CostEstimate(
            flops=4500000000, bytes_accessed=20000000, transcendentals=350000
        ),
        name="feed",
    )(attn, states, ffn_gain.reshape(1, 4096), w_out, w_all, w_down)
    return out.reshape(8, 48, 128)


def solution(mesh):
    return jax.shard_map(
        per_device,
        mesh=mesh,
        in_specs=(
            P("ctx", None),
            P(),
            P("cand", "mp", None),
            P("cand", "mp", None),
            P("ctx", "mp", None),
            P("ctx"),
            P(),
            P("cand", None),
            P(None, ("cand", "mp")),
            P(),
            P(None, "ctx", ("cand", "mp")),
            P(("cand", "mp"), None),
        ),
        out_specs=P(None, "ctx", ("cand", "mp")),
        check_vma=False,
    )
```

```python
import functools
import math

import jax
import jax.numpy as jnp
from jax import lax
from jax.experimental import pallas as pl
from jax.experimental.pallas import tpu as pltpu
from jax.sharding import PartitionSpec as P

EPSILON = 1e-05
ROPE_BASE = 500000.0
MESH = pl.DeviceIdType.MESH
F32 = jnp.float32
BF16 = jnp.bfloat16
DMA = pltpu.SemaphoreType.DMA
VM = pltpu.VMEM


def position():
    c = lax.axis_index("cand")
    s = lax.axis_index("ctx")
    m = lax.axis_index("mp")
    return c // 2, c % 2, s // 2, s % 2, m


def dev(x, k, y, h, m):
    return {"cand": x * 2 + k, "ctx": y * 2 + h, "mp": m}


def up(value, step, size=4):
    return lax.rem(value + step, size)


def remote(src, dst, send_sem, recv_sem, target):
    return pltpu.make_async_remote_copy(
        src_ref=src,
        dst_ref=dst,
        send_sem=send_sem,
        recv_sem=recv_sem,
        device_id=target,
        device_id_type=MESH,
    )


def greet(peers):
    barrier = pltpu.get_barrier_semaphore()
    for peer in peers:
        pl.semaphore_signal(barrier, inc=1, device_id=peer, device_id_type=MESH)
    pl.semaphore_wait(barrier, len(peers))


def turn(values, cosine, sine):
    return values * cosine + pltpu.roll(values, 64, 1) * sine


class Ring:
    def __init__(self, go, me, at, twin, view, send_sem, recv_sem, twin_send, twin_recv):
        self.go, self.me, self.at, self.twin, self.view = go, me, at, twin, view
        self.ss, self.rs, self.ts, self.tr = send_sem, recv_sem, twin_send, twin_recv

    def copy(self, src, dst, kind, part, step):
        return remote(src, dst, self.ss.at[kind, part], self.rs.at[kind, part], self.at(up(self.me, step)))

    def send(self, part, src):
        dst = self.view(self.me, part)
        steps = (1, 3) if part % 2 == 0 else (3, 1)
        for step in steps:
            self.go(self.copy(src, dst, 0 if step == 1 else 1, part, step))

    def take(self, kind, part):
        ref = self.view(up(self.me, (3, 1, 2)[kind]), part)
        self.copy(ref, ref, kind, part, 1).wait_recv()
        self.go(remote(ref, ref, self.ts.at[kind, part], self.tr.at[kind, part], self.twin))
        return ref

    def forward(self, part):
        ref = self.take(part % 2, part)
        self.go(self.copy(ref, ref, 2, part, 1 if part % 2 == 0 else 3))

    def collect(self, part):
        self.take(1 - part % 2, part)
        self.take(2, part)

    def done(self):
        for kind in range(3):
            for part in range(4):
                ref = self.view(up(self.me, (3, 1, 2)[kind]), part)
                remote(ref, ref, self.ts.at[kind, part], self.tr.at[kind, part], self.twin).wait_recv()


def layer_kernel(
    part,
    key_cos,
    key_sin,
    new_cos,
    new_sin,
    kv,
    flags,
    states,
    gain,
    w_shard,
    w_out,
    w_down,
    out,
    rs_in,
    q_own,
    n_own,
    q_all,
    n_all,
    kv_far,
    flags_far,
    keys,
    vals,
    new_keys,
    new_vals,
    live,
    q_rot,
    num_out,
    num_in,
    num_own,
    den_out,
    den_in,
    den_own,
    attn_all,
    out_w,
    gate_up_w,
    down_w,
    resid,
    shards,
    normed,
    acc,
    inner,
    x_out,
    x_in,
    x_own,
    z_out,
    z_in,
    swap_out,
    swap_in,
    rs_s,
    rs_r,
    q_s,
    q_r,
    n_s,
    n_r,
    kz_s,
    kz_r,
    kf_s,
    kf_r,
    fl_s,
    fl_r,
    num_s,
    num_r,
    den_s,
    den_r,
    wz_s,
    wz_r,
    ring_s,
    ring_r,
    tw_s,
    tw_r,
    core_s,
    core_r,
    az_s,
    az_r,
    ax_s,
    ax_r,
    gz_s,
    gz_r,
    gx_s,
    gx_r,
    rx_s,
    rx_r,
    rz_s,
    rz_r,
    sw_s,
    sw_r,
    loc,
):
    x, k, y, h, m = position()
    c = x * 2 + k
    far = 1 - h
    cand_peers = [(x, 1 - k)] + [(up(x, i), kk) for i in (1, 2, 3) for kk in (k, 1 - k)]
    xy_peers = [(up(x, i), up(y, j)) for j in range(4) for i in range(4) if i or j]
    zhi = dev(x, k, y, far, m)
    x_peers = [up(x, i) for i in (1, 2, 3)]
    m_peers = [up(m, i) for i in (1, 2, 3)]
    twin = dev(x, 1 - k, y, h, m)
    near_s = 2 * y + h
    far_s = 2 * y + far

    def at_x(a):
        return dev(a, k, y, h, m)

    def at_y(a):
        return dev(x, k, a, h, m)

    def at_m(a):
        return dev(x, k, y, h, a)

    greet(
        [dev(a, b, y, h, m) for a, b in cand_peers]
        + [dev(a, k, b, h, m) for a, b in xy_peers[3:]]
        + [dev(up(x, i), k, y, far, m) for i in range(4)]
        + [at_m(a) for a in m_peers]
    )
    rows = kv_far.shape[1]
    sends = []

    def go(copy):
        copy.start()
        sends.append(copy)
        return copy

    for i, (a, b) in enumerate(cand_peers):
        go(remote(part.at[a], rs_in.at[i], rs_s.at[i], rs_r.at[i], dev(a, b, y, h, m)))
    mine = kv.at[pl.ds(pl.multiple_of(c * rows, 16), rows)]
    kz = go(remote(mine, kv_far.at[c], kz_s, kz_r, zhi))
    fl = go(remote(flags, flags_far, fl_s, fl_r, zhi))
    side = pl.ds(pl.multiple_of(k * 128, 128), 128)
    pairs = [
        (w_out, out_w.at[:, side]),
        (w_shard, gate_up_w.at[k, near_s]),
        (w_down, down_w.at[k]),
    ]
    local = []
    shared = []
    for i, (src, dst) in enumerate(pairs):
        copy = pltpu.make_async_copy(src, dst, loc.at[i])
        copy.start()
        local.append(copy)
        shared.append(go(remote(src, dst, core_s.at[i], core_r.at[i], twin)))

    def near_view(b, part):
        return gate_up_w.at[k, 2 * b + h, pl.ds(part * 224, 224)]

    def far_view(b, part):
        return gate_up_w.at[k, 2 * b + far, pl.ds(part * 224, 224)]

    near_ring = Ring(go, y, at_y, twin, near_view, ring_s.at[0], ring_r.at[0], tw_s.at[0], tw_r.at[0])
    far_ring = Ring(go, y, at_y, twin, far_view, ring_s.at[1], ring_r.at[1], tw_s.at[1], tw_r.at[1])

    def send_near(p):
        near_ring.send(p, w_shard.at[pl.ds(p * 224, 224)])

    def send_far(p):
        go(remote(w_shard.at[pl.ds(p * 224, 224)], near_view(y, p), wz_s.at[p], wz_r.at[p], zhi))

    def take_far(p):
        ref = far_view(y, p)
        remote(ref, ref, wz_s.at[p], wz_r.at[p], zhi).wait_recv()
        go(remote(ref, ref, core_s.at[3 + p], core_r.at[3 + p], twin))
        far_ring.send(p, ref)

    for p in (0,):
        send_near(p)
    send_near(1)
    half = kv.shape[0]

    def place(block, where, source):
        for j in range(2):
            raw = source[:, j * 256 : j * 256 + 128].astype(F32)
            keys[j, where, :] = turn(raw, block[0], block[1]).astype(BF16)
            vals[j, where, :] = source[:, j * 256 + 128 : j * 256 + 256]

    place((key_cos[0], key_sin[0]), pl.ds(0, half), kv[...])
    for j in range(2):
        new_keys[j] = jnp.zeros(new_keys.shape[1:], BF16)
        new_vals[j] = jnp.zeros(new_vals.shape[1:], BF16)

    for i, (a, b) in enumerate(cand_peers):
        remote(part.at[a], rs_in.at[i], rs_s.at[i], rs_r.at[i], dev(a, b, y, h, m)).wait_recv()
    total = part[x].astype(F32)
    for i in range(7):
        total = total + rs_in[i].astype(F32)
    summed = total.astype(BF16)
    q_own[...] = summed[:, :256]
    n_own[...] = summed[:, 256:]
    q_all[y, x] = summed[:, :256]
    n_all[0, x] = summed[:, 256:]
    for i, (a, b) in enumerate(xy_peers):
        go(remote(q_own, q_all.at[y, x], q_s.at[i], q_r.at[i], dev(a, k, b, h, m)))
    for i in (1, 2, 3):
        go(remote(n_own, n_all.at[0, x], n_s.at[i], n_r.at[i], dev(up(x, i), k, y, h, m)))
    for i in range(4):
        go(remote(n_own, n_all.at[1, x], n_s.at[4 + i], n_r.at[4 + i], dev(up(x, i), k, y, far, m)))

    for p in (0, 1):
        send_far(p)
    for p in (2, 3):
        send_near(p)
    kz.wait_recv()
    for i, (a, b) in enumerate(cand_peers):
        go(remote(kv_far.at[c], kv_far.at[c], kf_s.at[i], kf_r.at[i], dev(a, b, y, h, m)))
    fl.wait_recv()
    for page in range(6):
        live[:, page * 128 : page * 128 + 128] = jnp.broadcast_to(flags[:, page : page + 1], (8, 128))
        live[:, half + page * 128 : half + page * 128 + 128] = jnp.broadcast_to(
            flags_far[:, page : page + 1], (8, 128)
        )

    for i, (a, b) in enumerate(xy_peers):
        remote(q_own, q_all.at[b, a], q_s.at[i], q_r.at[i], dev(a, k, b, h, m)).wait_recv()

    def turn_queries(b, carry):
        cosine = new_cos[2 * b + h]
        sine = new_sin[2 * b + h]
        for head in range(8):
            raw = q_all[b, head // 2, :, (head % 2) * 128 : (head % 2) * 128 + 128].astype(F32)
            spot = (head % 4) * 48
            q_rot[head // 4, b, spot : spot + 48, :] = turn(raw, cosine, sine).astype(BF16)
        return carry

    lax.fori_loop(0, 4, turn_queries, 0)

    for i in (1, 2, 3):
        remote(n_own, n_all.at[0, x], n_s.at[i], n_r.at[i], zhi).wait_recv()
    for i in range(4):
        remote(n_own, n_all.at[1, x], n_s.at[4 + i], n_r.at[4 + i], zhi).wait_recv()
    for block in range(2):
        owner = 2 * y + (h if block == 0 else far)
        for j in range(2):
            raw = n_all[block, 2 * j].astype(F32)
            spot = block * 48
            new_keys[j, spot : spot + 48, :] = turn(raw, new_cos[owner], new_sin[owner]).astype(BF16)
            new_vals[j, spot : spot + 48, :] = n_all[block, 2 * j + 1]

    for i, (a, b) in enumerate(cand_peers):
        remote(
            kv_far.at[c], kv_far.at[a * 2 + b], kf_s.at[i], kf_r.at[i], dev(a, b, y, h, m)
        ).wait_recv()
    place(
        (key_cos[1], key_sin[1]),
        pl.ds(half, half),
        kv_far[...].reshape(half, kv.shape[1]),
    )

    scale = 128 ** (-0.5)
    lane = lax.broadcasted_iota(jnp.int32, (48, 128), 1)
    key_lane = lax.broadcasted_iota(jnp.int32, (192, 128), 1)
    token = lax.broadcasted_iota(jnp.int32, (4, 48, 128), 1).reshape(192, 128)
    first = (2 * y + h) * 48
    second = (2 * y + far) * 48
    key_index = jnp.where(
        key_lane < 48, first + key_lane, jnp.where(key_lane < 96, second + key_lane - 48, 1 << 20)
    )
    nt = (((1,), (1,)), ((), ()))

    def attend(step, carry):
        j = step // 4
        i = step % 4
        b = up(y, i + 1)
        query = q_rot[j, b]
        scores = lax.dot_general(query, keys[j], nt, preferred_element_type=F32)
        expo = jnp.where(live[0:1, :] > 0.5, jnp.exp(scores * scale), 0.0)
        recent = lax.dot_general(query, new_keys[j], nt, preferred_element_type=F32)
        seen = key_index <= (2 * b + h) * 48 + token
        recent_expo = jnp.where(seen, jnp.exp(recent * scale), 0.0)
        denom = jnp.sum(expo, axis=1, keepdims=True) + jnp.sum(recent_expo, axis=1, keepdims=True)
        numer = jnp.dot(expo.astype(BF16), vals[j], preferred_element_type=F32)
        numer = numer + jnp.dot(recent_expo.astype(BF16), new_vals[j], preferred_element_type=F32)
        lanes = jnp.zeros((48, 128), F32)
        for g in range(4):
            lanes = lanes + jnp.where(lane == j * 4 + g, denom[g * 48 : g * 48 + 48], 0.0)

        @pl.when(i < 3)
        def _():
            num_out[j, i] = numer.astype(BF16)
            remote(
                num_out.at[j, i], num_in.at[j, i], num_s.at[j, i], num_r.at[j, i], dev(x, k, b, h, m)
            ).start()

            @pl.when(j == 0)
            def _():
                den_out[i] = lanes

            @pl.when(j == 1)
            def _():
                den_out[i] = den_out[i] + lanes
                remote(
                    den_out.at[i], den_in.at[i], den_s.at[i], den_r.at[i], dev(x, k, b, h, m)
                ).start()

        @pl.when(i == 3)
        def _():
            num_own[j] = numer

            @pl.when(j == 0)
            def _():
                den_own[...] = lanes

            @pl.when(j == 1)
            def _():
                den_own[...] = den_own[...] + lanes

        return carry

    lax.fori_loop(0, 8, attend, 0)
    send_far(2)
    for p in range(4):
        near_ring.forward(p)
    for p in (0, 1):
        take_far(p)

    denom = den_own[...]
    for i in range(3):
        copy = remote(den_out.at[i], den_in.at[i], den_s.at[i], den_r.at[i], dev(x, k, up(y, i + 1), h, m))
        copy.wait()
        denom = denom + den_in[i]
    for j in range(2):
        numer = num_own[j]
        for i in range(3):
            remote(
                num_out.at[j, i],
                num_in.at[j, i],
                num_s.at[j, i],
                num_r.at[j, i],
                dev(x, k, up(y, i + 1), h, m),
            ).wait()
            numer = numer + num_in[j, i].astype(F32)
        for g in range(4):
            head = j * 4 + g
            attn_all[m, pl.ds(pl.multiple_of(x * 48, 16), 48), head * 128 : head * 128 + 128] = (
                numer[g * 48 : g * 48 + 48] / denom[:, head : head + 1]
            ).astype(BF16)


    def gather(view, zs, zr, xs, xr):
        own = view(x, m)
        for i, b in enumerate(m_peers):
            go(remote(own, own, zs.at[i], zr.at[i], at_m(b)))
        for j, a in enumerate(x_peers):
            go(remote(own, own, xs.at[3, j], xr.at[3, j], at_x(a)))
        for i in range(3):
            came = view(x, up(m, 3 - i))
            remote(own, came, zs.at[i], zr.at[i], at_m(m_peers[i])).wait_recv()
            for j, a in enumerate(x_peers):
                go(remote(came, came, xs.at[i, j], xr.at[i, j], at_x(a)))

    def gather_rest(view, xs, xr):
        for i in (3, 0, 1, 2):
            for j in range(3):
                came = view(up(x, 3 - j), up(m, 3 - i) if i < 3 else m)
                remote(came, came, xs.at[i, j], xr.at[i, j], at_x(x_peers[j])).wait_recv()

    def attn_view(a, b):
        return attn_all.at[b, pl.ds(pl.multiple_of(a * 48, 16), 48)]

    gather(attn_view, az_s, az_r, ax_s, ax_r)
    send_far(3)
    for p in range(4):
        near_ring.collect(p)
    take_far(2)
    for p in (0, 1):
        far_ring.forward(p)
    gather_rest(attn_view, ax_s, ax_r)
    local[0].wait()
    shared[0].wait_recv()

    total = jnp.dot(attn_all[0], out_w[0:1024, :], preferred_element_type=F32)
    for b in range(1, 4):
        total = total + jnp.dot(
            attn_all[b], out_w[b * 1024 : b * 1024 + 1024, :], preferred_element_type=F32
        )
    even = pl.ds(pl.multiple_of((8 * x + m) * 128, 128), 128)
    odd = pl.ds(pl.multiple_of((8 * x + 4 + m) * 128, 128), 128)
    columns = jnp.concatenate([states[:, even], states[:, odd]], axis=1).astype(F32)
    gains = jnp.concatenate([gain[:, even], gain[:, odd]], axis=1)
    kept = total + jnp.concatenate([columns] * 4, axis=0)
    resid[...] = kept

    def shard_view(a, b):
        return shards.at[a, b]

    shards[x, m] = (kept * gains).astype(BF16)
    gather(shard_view, gz_s, gz_r, gx_s, gx_r)

    take_far(3)
    far_ring.forward(2)
    gather_rest(shard_view, gx_s, gx_r)
    far_ring.forward(3)
    for p in range(4):
        far_ring.collect(p)

    squares = jnp.zeros((192, 128), F32)
    for a in range(4):
        for b in range(4):
            for e in range(2):
                block = shards[a, b, :, e * 128 : e * 128 + 128]
                normed[2 * a + e, :, b * 128 : b * 128 + 128] = block
                spot = (8 * a + 4 * e + b) * 128
                plain = block.astype(F32) / gain[:, spot : spot + 128]
                squares = squares + plain * plain
    ratio = lax.rsqrt(jnp.sum(squares, axis=1, keepdims=True) / 4096 + EPSILON)

    for copy in local[1:]:
        copy.wait()
    for copy in shared[1:]:
        copy.wait_recv()
    for p in range(4):
        ref = gate_up_w.at[1 - k, far_s, pl.ds(p * 224, 224)]
        remote(ref, ref, core_s.at[3 + p], core_r.at[3 + p], twin).wait_recv()
    near_ring.done()
    far_ring.done()

    acc[...] = jnp.zeros(acc.shape, F32)

    def gate_up(s, carry):
        for cc in range(2):
            for part in range(2):
                acc[cc, part] = acc[cc, part] + lax.dot_general(
                    normed[s],
                    gate_up_w[cc, s, part * 448 : part * 448 + 448, :],
                    nt,
                    preferred_element_type=F32,
                )
        return carry

    lax.fori_loop(0, 8, gate_up, 0)
    for cc in range(2):
        gate = acc[cc, 0] * ratio
        upward = acc[cc, 1] * ratio
        inner[cc] = (gate / (1.0 + jnp.exp(-gate)) * upward).astype(BF16)

    def down(step, carry):
        zi = step // 4
        xi = step % 4
        b = up(m, zi + 1)
        a = up(x, xi + 1)
        first = pl.ds(pl.multiple_of((8 * a + b) * 128, 128), 128)
        second = pl.ds(pl.multiple_of((8 * a + 4 + b) * 128, 128), 128)
        block = jnp.zeros((192, 256), F32)
        for cc in range(2):
            weights = jnp.concatenate([down_w[cc, :, first], down_w[cc, :, second]], axis=1)
            block = block + jnp.dot(inner[cc], weights, preferred_element_type=F32)

        @pl.when(xi < 3)
        def _():
            x_out[xi, zi] = block.astype(BF16)
            remote(
                x_out.at[xi, zi], x_in.at[xi, zi], rx_s.at[xi, zi], rx_r.at[xi, zi], at_x(a)
            ).start()

        @pl.when(xi == 3)
        def _():
            x_own[zi] = block

        return carry

    lax.fori_loop(0, 16, down, 0)
    for zi in range(4):
        block = x_own[zi]
        for xi in range(3):
            remote(
                x_out.at[xi, zi], x_in.at[xi, zi], rx_s.at[xi, zi], rx_r.at[xi, zi], at_x(x_peers[xi])
            ).wait()
            block = block + x_in[xi, zi].astype(F32)
        if zi < 3:
            z_out[zi] = block.astype(BF16)
            go(remote(z_out.at[zi], z_in.at[zi], rz_s.at[zi], rz_r.at[zi], at_m(m_peers[zi])))
    block = block + resid[...]
    for zi in range(3):
        remote(z_out.at[zi], z_in.at[zi], rz_s.at[zi], rz_r.at[zi], at_m(m_peers[zi])).wait_recv()
        block = block + z_in[zi].astype(F32)
    result = block.astype(BF16)
    lower = result[:, :128]
    upper = result[:, 128:]
    swap_out[...] = jnp.where(k == 0, upper, lower)
    swap = go(remote(swap_out, swap_in, sw_s, sw_r, twin))
    kept_half = jnp.where(k == 0, lower, upper)
    for a in range(4):
        out[a, k] = kept_half[a * 48 : a * 48 + 48]
    swap.wait_recv()
    for a in range(4):
        out[a, 1 - k] = swap_in[a * 48 : a * 48 + 48, :]
    for copy in sends:
        copy.wait_send()


def rms_scale(values, gain):
    return values * lax.rsqrt(jnp.mean(values * values, axis=-1, keepdims=True) + EPSILON) * gain


def base_freq(half):
    steps = jnp.arange(half, dtype=F32)
    return jnp.exp(steps * (-2.0 * math.log(ROPE_BASE) / (2 * half)))


def tables(where, freq):
    angle = where.astype(F32)[:, None] * freq[None, :]
    cosine = jnp.cos(angle)
    sine = jnp.sin(angle)
    return jnp.concatenate([cosine, cosine], axis=1), jnp.concatenate([-sine, sine], axis=1)


def per_device(
    states,
    attn_gain,
    w_query,
    w_keyval,
    kv_cache,
    page_live,
    factor_levels,
    cand_index,
    w_out,
    ffn_gain,
    w_gate_up,
    w_down,
):
    x, k, y, h, m = position()
    c = lax.axis_index("cand")
    normed = rms_scale(states.astype(F32), attn_gain).astype(BF16)
    slab = lax.dynamic_slice_in_dim(normed, c * 512, 512, 1)
    query_part = jnp.einsum("td,dkc->tkc", slab, w_query, preferred_element_type=F32)
    keyval_part = jnp.einsum("td,dkc->tkc", slab, w_keyval, preferred_element_type=F32)
    part = jnp.concatenate(
        [query_part.reshape(48, 4, 256), keyval_part.reshape(48, 4, 128)], axis=2
    ).astype(BF16)
    part = jnp.transpose(part, (1, 0, 2))
    picks = (cand_index[0][:, None] == jnp.arange(16, dtype=jnp.int32)[None, :]).astype(F32)
    factors = jnp.sum(picks * factor_levels[None, :], axis=-1)
    freq = base_freq(64) / factors
    spots = jnp.arange(768, dtype=jnp.int32)
    near = (2 * y + h) * 768 + spots
    far = (2 * y + 1 - h) * 768 + spots
    key_cos, key_sin = tables(jnp.concatenate([near, far]), freq)
    new_cos, new_sin = tables(6144 + jnp.arange(384, dtype=jnp.int32), freq)
    flags = jnp.pad((page_live == 1).astype(F32), (0, 122))
    flags = jnp.broadcast_to(flags[None, :], (8, 128))
    w_shard = jnp.swapaxes(w_gate_up, 1, 2).reshape(896, 512)

    vmem = pl.BlockSpec(memory_space=pltpu.VMEM)
    hbm = pl.BlockSpec(memory_space=pl.ANY)
    out = pl.pallas_call(
        layer_kernel,
        out_shape=jax.ShapeDtypeStruct((4, 2, 48, 128), BF16),
        in_specs=[vmem] * 9 + [hbm] * 3,
        out_specs=vmem,
        scratch_shapes=[
            VM((7, 48, 384), BF16),
            VM((48, 256), BF16),
            VM((48, 128), BF16),
            VM((4, 4, 48, 256), BF16),
            VM((2, 4, 48, 128), BF16),
            VM((8, 96, 512), BF16),
            VM((8, 128), F32),
            VM((2, 1536, 128), BF16),
            VM((2, 1536, 128), BF16),
            VM((2, 128, 128), BF16),
            VM((2, 128, 128), BF16),
            VM((8, 1536), F32),
            VM((2, 4, 192, 128), BF16),
            VM((2, 3, 192, 128), BF16),
            VM((2, 3, 192, 128), BF16),
            VM((2, 192, 128), F32),
            VM((3, 48, 128), F32),
            VM((3, 48, 128), F32),
            VM((48, 128), F32),
            VM((4, 192, 1024), BF16),
            VM((4096, 256), BF16),
            VM((2, 8, 896, 512), BF16),
            VM((2, 448, 4096), BF16),
            VM((192, 256), F32),
            VM((4, 4, 192, 256), BF16),
            VM((8, 192, 512), BF16),
            VM((2, 2, 192, 448), F32),
            VM((2, 192, 448), BF16),
            VM((3, 4, 192, 256), BF16),
            VM((3, 4, 192, 256), BF16),
            VM((4, 192, 256), F32),
            VM((3, 192, 256), BF16),
            VM((3, 192, 256), BF16),
            VM((192, 128), BF16),
            VM((192, 128), BF16),
            DMA((7,)),
            DMA((7,)),
            DMA((15,)),
            DMA((15,)),
            DMA((8,)),
            DMA((8,)),
            DMA,
            DMA,
            DMA((7,)),
            DMA((7,)),
            DMA,
            DMA,
            DMA((2, 3)),
            DMA((2, 3)),
            DMA((3,)),
            DMA((3,)),
            DMA((4,)),
            DMA((4,)),
            DMA((2, 3, 4)),
            DMA((2, 3, 4)),
            DMA((2, 3, 4)),
            DMA((2, 3, 4)),
            DMA((7,)),
            DMA((7,)),
            DMA((3,)),
            DMA((3,)),
            DMA((4, 3)),
            DMA((4, 3)),
            DMA((3,)),
            DMA((3,)),
            DMA((4, 3)),
            DMA((4, 3)),
            DMA((3, 4)),
            DMA((3, 4)),
            DMA((3,)),
            DMA((3,)),
            DMA,
            DMA,
            DMA((3,)),
        ],
        compiler_params=pltpu.CompilerParams(
            collective_id=0, has_side_effects=True, vmem_limit_bytes=60 << 20
        ),
        name="layer",
    )(
        part,
        key_cos.reshape(2, 768, 128),
        key_sin.reshape(2, 768, 128),
        new_cos.reshape(8, 48, 128),
        new_sin.reshape(8, 48, 128),
        kv_cache.reshape(768, 512),
        flags,
        states,
        ffn_gain.reshape(1, 4096),
        w_shard,
        w_out,
        w_down,
    )
    return out.reshape(8, 48, 128)


def solution(mesh):
    return jax.shard_map(
        per_device,
        mesh=mesh,
        in_specs=(
            P("ctx", None),
            P(),
            P("cand", "mp", None),
            P("cand", "mp", None),
            P("ctx", "mp", None),
            P("ctx"),
            P(),
            P("cand", None),
            P(None, ("cand", "mp")),
            P(),
            P(None, "ctx", ("cand", "mp")),
            P(("cand", "mp"), None),
        ),
        out_specs=P(None, "ctx", ("cand", "mp")),
        check_vma=False,
    )
```

```python
import functools
import math

import jax
import jax.numpy as jnp
from jax import lax
from jax.experimental import pallas as pl
from jax.experimental.pallas import tpu as pltpu
from jax.sharding import PartitionSpec as P

EPSILON = 1e-05
ROPE_BASE = 500000.0
MESH = pl.DeviceIdType.MESH
F32 = jnp.float32
BF16 = jnp.bfloat16
DMA = pltpu.SemaphoreType.DMA
VM = pltpu.VMEM


def position():
    c = lax.axis_index("cand")
    s = lax.axis_index("ctx")
    m = lax.axis_index("mp")
    return c // 2, c % 2, s // 2, s % 2, m


def dev(x, k, y, h, m):
    return {"cand": x * 2 + k, "ctx": y * 2 + h, "mp": m}


def up(value, step, size=4):
    return lax.rem(value + step, size)


def remote(src, dst, send_sem, recv_sem, target):
    return pltpu.make_async_remote_copy(
        src_ref=src,
        dst_ref=dst,
        send_sem=send_sem,
        recv_sem=recv_sem,
        device_id=target,
        device_id_type=MESH,
    )


def greet(peers):
    barrier = pltpu.get_barrier_semaphore()
    for peer in peers:
        pl.semaphore_signal(barrier, inc=1, device_id=peer, device_id_type=MESH)
    pl.semaphore_wait(barrier, len(peers))


def turn(values, cosine, sine):
    return values * cosine + pltpu.roll(values, 64, 1) * sine


class Ring:
    def __init__(self, go, me, at, twin, view, send_sem, recv_sem, twin_send, twin_recv):
        self.go, self.me, self.at, self.twin, self.view = go, me, at, twin, view
        self.ss, self.rs, self.ts, self.tr = send_sem, recv_sem, twin_send, twin_recv

    def copy(self, src, dst, kind, part, step):
        return remote(src, dst, self.ss.at[kind, part], self.rs.at[kind, part], self.at(up(self.me, step)))

    def send(self, part, src):
        dst = self.view(self.me, part)
        steps = (1, 3) if part % 2 == 0 else (3, 1)
        for step in steps:
            self.go(self.copy(src, dst, 0 if step == 1 else 1, part, step))

    def take(self, kind, part):
        ref = self.view(up(self.me, (3, 1, 2)[kind]), part)
        self.copy(ref, ref, kind, part, 1).wait_recv()
        self.go(remote(ref, ref, self.ts.at[kind, part], self.tr.at[kind, part], self.twin))
        return ref

    def forward(self, part):
        ref = self.take(part % 2, part)
        self.go(self.copy(ref, ref, 2, part, 1 if part % 2 == 0 else 3))

    def collect(self, part):
        self.take(1 - part % 2, part)
        self.take(2, part)

    def done(self):
        for kind in range(3):
            for part in range(4):
                ref = self.view(up(self.me, (3, 1, 2)[kind]), part)
                remote(ref, ref, self.ts.at[kind, part], self.tr.at[kind, part], self.twin).wait_recv()


def layer_kernel(
    part,
    cosines,
    sines,
    kv,
    flags,
    states,
    gain,
    w_shard,
    w_out,
    w_down,
    out,
    rs_in,
    q_own,
    n_own,
    q_all,
    n_all,
    kv_far,
    flags_far,
    keys,
    vals,
    new_keys,
    new_vals,
    live,
    q_rot,
    num_out,
    num_in,
    num_own,
    den_out,
    den_in,
    den_own,
    attn_all,
    out_w,
    gate_up_w,
    down_w,
    resid,
    shards,
    normed,
    acc,
    inner,
    x_out,
    x_in,
    x_own,
    z_out,
    z_in,
    swap_out,
    swap_in,
    rs_s,
    rs_r,
    q_s,
    q_r,
    n_s,
    n_r,
    kz_s,
    kz_r,
    kf_s,
    kf_r,
    kt_s,
    kt_r,
    qt_s,
    qt_r,
    fl_s,
    fl_r,
    num_s,
    num_r,
    den_s,
    den_r,
    wz_s,
    wz_r,
    ring_s,
    ring_r,
    tw_s,
    tw_r,
    core_s,
    core_r,
    az_s,
    az_r,
    ax_s,
    ax_r,
    gz_s,
    gz_r,
    gx_s,
    gx_r,
    rx_s,
    rx_r,
    rz_s,
    rz_r,
    sw_s,
    sw_r,
    loc,
):
    x, k, y, h, m = position()
    c = x * 2 + k
    far = 1 - h
    cand_peers = [(x, 1 - k)] + [(up(x, i), kk) for i in (1, 2, 3) for kk in (k, 1 - k)]
    xy_peers = [(up(x, i), up(y, j)) for j in range(4) for i in range(4) if i or j]
    zhi = dev(x, k, y, far, m)
    x_peers = [up(x, i) for i in (1, 2, 3)]
    m_peers = [up(m, i) for i in (1, 2, 3)]
    twin = dev(x, 1 - k, y, h, m)
    near_s = 2 * y + h
    far_s = 2 * y + far

    def at_x(a):
        return dev(a, k, y, h, m)

    def at_y(a):
        return dev(x, k, a, h, m)

    def at_m(a):
        return dev(x, k, y, h, a)

    greet(
        [dev(a, b, y, h, m) for a, b in cand_peers]
        + [dev(a, k, b, h, m) for a, b in xy_peers[3:]]
        + [dev(up(x, i), k, y, far, m) for i in range(4)]
        + [at_m(a) for a in m_peers]
    )
    rows = kv_far.shape[1]
    sends = []

    def go(copy):
        copy.start()
        sends.append(copy)
        return copy

    for i, (a, b) in enumerate(cand_peers):
        go(remote(part.at[2 * a + b], rs_in.at[i], rs_s.at[i], rs_r.at[i], dev(a, b, y, h, m)))
    mine = kv.at[pl.ds(pl.multiple_of(c * rows, 16), rows)]
    kz = go(remote(mine, kv_far.at[c], kz_s, kz_r, zhi))
    fl = go(remote(flags, flags_far, fl_s, fl_r, zhi))
    side = pl.ds(pl.multiple_of(k * 128, 128), 128)
    pairs = [
        (w_out, out_w.at[:, side]),
        (w_shard, gate_up_w.at[k, near_s]),
        (w_down, down_w.at[k]),
    ]
    local = []
    shared = []
    for i, (src, dst) in enumerate(pairs):
        copy = pltpu.make_async_copy(src, dst, loc.at[i])
        copy.start()
        local.append(copy)
        shared.append(go(remote(src, dst, core_s.at[i], core_r.at[i], twin)))

    def near_view(b, part):
        return gate_up_w.at[k, 2 * b + h, pl.ds(part * 224, 224)]

    def far_view(b, part):
        return gate_up_w.at[k, 2 * b + far, pl.ds(part * 224, 224)]

    near_ring = Ring(go, y, at_y, twin, near_view, ring_s.at[0], ring_r.at[0], tw_s.at[0], tw_r.at[0])
    far_ring = Ring(go, y, at_y, twin, far_view, ring_s.at[1], ring_r.at[1], tw_s.at[1], tw_r.at[1])

    def send_near(p):
        near_ring.send(p, w_shard.at[pl.ds(p * 224, 224)])

    def send_far(p):
        go(remote(w_shard.at[pl.ds(p * 224, 224)], near_view(y, p), wz_s.at[p], wz_r.at[p], zhi))

    def take_far(p):
        ref = far_view(y, p)
        remote(ref, ref, wz_s.at[p], wz_r.at[p], zhi).wait_recv()
        go(remote(ref, ref, core_s.at[3 + p], core_r.at[3 + p], twin))
        far_ring.send(p, ref)

    for p in (0,):
        send_near(p)
    send_near(1)
    half = kv.shape[0]

    sign = jnp.where(lax.broadcasted_iota(jnp.int32, (1, 128), 1) < 64, -1.0, 1.0)

    def angles(base, count):
        first_cos = cosines[pl.ds(base, 1), :]
        first_sin = sines[pl.ds(base, 1), :]
        place_cos = cosines[pl.ds(0, count), :]
        place_sin = sines[pl.ds(0, count), :]
        return (
            first_cos * place_cos - first_sin * place_sin,
            (first_sin * place_cos + first_cos * place_sin) * sign,
        )

    def place_page(side, page, source):
        cosine, sine = angles(128 + side * 6 + page, 128)
        rows = pl.ds(side * half + page * 128, 128)
        for j in range(2):
            raw = source[:, j * 256 : j * 256 + 128].astype(F32)
            keys[j, rows, :] = turn(raw, cosine, sine).astype(BF16)
            vals[j, rows, :] = source[:, j * 256 + 128 : j * 256 + 256]

    for page in range(6):
        place_page(0, page, kv[page * 128 : page * 128 + 128, :])
    for j in range(2):
        new_keys[j] = jnp.zeros(new_keys.shape[1:], BF16)
        new_vals[j] = jnp.zeros(new_vals.shape[1:], BF16)

    for i, (a, b) in enumerate(cand_peers):
        remote(part.at[c], rs_in.at[i], rs_s.at[i], rs_r.at[i], dev(a, b, y, h, m)).wait_recv()
    total = part[c].astype(F32)
    for i in range(7):
        total = total + rs_in[i].astype(F32)
    summed = total.astype(BF16)
    q_own[...] = summed[:, :128]
    n_own[...] = summed[:, 128:]
    q_all[k, y, x] = summed[:, :128]
    n_all[0, x] = summed[:, 128:]
    for i, (a, b) in enumerate(xy_peers):
        go(remote(q_own, q_all.at[k, y, x], q_s.at[i], q_r.at[i], dev(a, k, b, h, m)))
    for i in (1, 2, 3):
        go(remote(n_own, n_all.at[0, x], n_s.at[i], n_r.at[i], dev(up(x, i), k, y, h, m)))
    for i in range(4):
        go(remote(n_own, n_all.at[1, x], n_s.at[4 + i], n_r.at[4 + i], dev(up(x, i), k, y, far, m)))

    for p in (0, 1):
        send_far(p)
    for p in (2, 3):
        send_near(p)
    kz.wait_recv()
    for i, a in enumerate(x_peers):
        go(remote(kv_far.at[c], kv_far.at[c], kf_s.at[i], kf_r.at[i], at_x(a)))
    go(remote(kv_far.at[c], kv_far.at[c], kt_s.at[3], kt_r.at[3], twin))
    fl.wait_recv()
    for page in range(6):
        live[:, page * 128 : page * 128 + 128] = jnp.broadcast_to(flags[:, page : page + 1], (8, 128))
        live[:, half + page * 128 : half + page * 128 + 128] = jnp.broadcast_to(
            flags_far[:, page : page + 1], (8, 128)
        )

    for i, (a, b) in enumerate(xy_peers):
        remote(q_own, q_all.at[k, b, a], q_s.at[i], q_r.at[i], dev(a, k, b, h, m)).wait_recv()
    pair = go(remote(q_all.at[k], q_all.at[k], qt_s, qt_r, twin))
    for i in (1, 2, 3):
        remote(n_own, n_all.at[0, x], n_s.at[i], n_r.at[i], zhi).wait_recv()
    for i in range(4):
        remote(n_own, n_all.at[1, x], n_s.at[4 + i], n_r.at[4 + i], zhi).wait_recv()
    for block in range(2):
        cosine, sine = angles(140 + 2 * y + (h if block == 0 else far), 48)
        for j in range(2):
            raw = n_all[block, 2 * j].astype(F32)
            spot = block * 48
            new_keys[j, spot : spot + 48, :] = turn(raw, cosine, sine).astype(BF16)
            new_vals[j, spot : spot + 48, :] = n_all[block, 2 * j + 1]
    pair.wait_recv()

    def turn_queries(b, carry):
        cosine, sine = angles(140 + 2 * b + h, 48)
        for head in range(8):
            raw = q_all[head % 2, b, head // 2].astype(F32)
            spot = (head % 4) * 48
            q_rot[head // 4, b, spot : spot + 48, :] = turn(raw, cosine, sine).astype(BF16)
        return carry

    lax.fori_loop(0, 4, turn_queries, 0)

    for i in range(3):
        came = kv_far.at[2 * up(x, 3 - i) + k]
        remote(came, came, kf_s.at[i], kf_r.at[i], twin).wait_recv()
        go(remote(came, came, kt_s.at[i], kt_r.at[i], twin))
    for i in range(4):
        came = kv_far.at[2 * up(x, 3 - i) + 1 - k]
        remote(came, came, kt_s.at[i], kt_r.at[i], twin).wait_recv()
    far_rows = kv_far[...].reshape(half, kv.shape[1])
    for page in range(6):
        place_page(1, page, far_rows[page * 128 : page * 128 + 128])

    scale = 128 ** (-0.5)
    lane = lax.broadcasted_iota(jnp.int32, (48, 128), 1)
    key_lane = lax.broadcasted_iota(jnp.int32, (192, 128), 1)
    token = lax.broadcasted_iota(jnp.int32, (4, 48, 128), 1).reshape(192, 128)
    first = (2 * y + h) * 48
    second = (2 * y + far) * 48
    key_index = jnp.where(
        key_lane < 48, first + key_lane, jnp.where(key_lane < 96, second + key_lane - 48, 1 << 20)
    )
    nt = (((1,), (1,)), ((), ()))

    def attend(step, carry):
        j = step // 4
        i = step % 4
        b = up(y, i + 1)
        query = q_rot[j, b]
        scores = lax.dot_general(query, keys[j], nt, preferred_element_type=F32)
        expo = jnp.where(live[0:1, :] > 0.5, jnp.exp(scores * scale), 0.0)
        recent = lax.dot_general(query, new_keys[j], nt, preferred_element_type=F32)
        seen = key_index <= (2 * b + h) * 48 + token
        recent_expo = jnp.where(seen, jnp.exp(recent * scale), 0.0)
        denom = jnp.sum(expo, axis=1, keepdims=True) + jnp.sum(recent_expo, axis=1, keepdims=True)
        numer = jnp.dot(expo.astype(BF16), vals[j], preferred_element_type=F32)
        numer = numer + jnp.dot(recent_expo.astype(BF16), new_vals[j], preferred_element_type=F32)
        lanes = jnp.zeros((48, 128), F32)
        for g in range(4):
            lanes = lanes + jnp.where(lane == j * 4 + g, denom[g * 48 : g * 48 + 48], 0.0)

        @pl.when(i < 3)
        def _():
            num_out[j, i] = numer.astype(BF16)
            remote(
                num_out.at[j, i], num_in.at[j, i], num_s.at[j, i], num_r.at[j, i], dev(x, k, b, h, m)
            ).start()

            @pl.when(j == 0)
            def _():
                den_out[i] = lanes

            @pl.when(j == 1)
            def _():
                den_out[i] = den_out[i] + lanes
                remote(
                    den_out.at[i], den_in.at[i], den_s.at[i], den_r.at[i], dev(x, k, b, h, m)
                ).start()

        @pl.when(i == 3)
        def _():
            num_own[j] = numer

            @pl.when(j == 0)
            def _():
                den_own[...] = lanes

            @pl.when(j == 1)
            def _():
                den_own[...] = den_own[...] + lanes

        return carry

    lax.fori_loop(0, 8, attend, 0)
    send_far(2)
    for p in range(4):
        near_ring.forward(p)
    for p in (0, 1):
        take_far(p)

    denom = den_own[...]
    for i in range(3):
        copy = remote(den_out.at[i], den_in.at[i], den_s.at[i], den_r.at[i], dev(x, k, up(y, i + 1), h, m))
        copy.wait()
        denom = denom + den_in[i]
    for j in range(2):
        numer = num_own[j]
        for i in range(3):
            remote(
                num_out.at[j, i],
                num_in.at[j, i],
                num_s.at[j, i],
                num_r.at[j, i],
                dev(x, k, up(y, i + 1), h, m),
            ).wait()
            numer = numer + num_in[j, i].astype(F32)
        for g in range(4):
            head = j * 4 + g
            attn_all[m, pl.ds(pl.multiple_of(x * 48, 16), 48), head * 128 : head * 128 + 128] = (
                numer[g * 48 : g * 48 + 48] / denom[:, head : head + 1]
            ).astype(BF16)


    def gather(view, zs, zr, xs, xr):
        own = view(x, m)
        for i, b in enumerate(m_peers):
            go(remote(own, own, zs.at[i], zr.at[i], at_m(b)))
        for j, a in enumerate(x_peers):
            go(remote(own, own, xs.at[3, j], xr.at[3, j], at_x(a)))
        for i in range(3):
            came = view(x, up(m, 3 - i))
            remote(own, came, zs.at[i], zr.at[i], at_m(m_peers[i])).wait_recv()
            for j, a in enumerate(x_peers):
                go(remote(came, came, xs.at[i, j], xr.at[i, j], at_x(a)))

    def gather_rest(view, xs, xr):
        for i in (3, 0, 1, 2):
            for j in range(3):
                came = view(up(x, 3 - j), up(m, 3 - i) if i < 3 else m)
                remote(came, came, xs.at[i, j], xr.at[i, j], at_x(x_peers[j])).wait_recv()

    def attn_view(a, b):
        return attn_all.at[b, pl.ds(pl.multiple_of(a * 48, 16), 48)]

    gather(attn_view, az_s, az_r, ax_s, ax_r)
    send_far(3)
    for p in range(4):
        near_ring.collect(p)
    take_far(2)
    for p in (0, 1):
        far_ring.forward(p)
    gather_rest(attn_view, ax_s, ax_r)
    local[0].wait()
    shared[0].wait_recv()

    total = jnp.dot(attn_all[0], out_w[0:1024, :], preferred_element_type=F32)
    for b in range(1, 4):
        total = total + jnp.dot(
            attn_all[b], out_w[b * 1024 : b * 1024 + 1024, :], preferred_element_type=F32
        )
    even = pl.ds(pl.multiple_of((8 * x + m) * 128, 128), 128)
    odd = pl.ds(pl.multiple_of((8 * x + 4 + m) * 128, 128), 128)
    columns = jnp.concatenate([states[:, even], states[:, odd]], axis=1).astype(F32)
    gains = jnp.concatenate([gain[:, even], gain[:, odd]], axis=1)
    kept = total + jnp.concatenate([columns] * 4, axis=0)
    resid[...] = kept

    def shard_view(a, b):
        return shards.at[a, b]

    shards[x, m] = (kept * gains).astype(BF16)
    gather(shard_view, gz_s, gz_r, gx_s, gx_r)

    take_far(3)
    far_ring.forward(2)
    gather_rest(shard_view, gx_s, gx_r)
    far_ring.forward(3)

    squares = jnp.zeros((192, 128), F32)
    for a in range(4):
        for b in range(4):
            for e in range(2):
                block = shards[a, b, :, e * 128 : e * 128 + 128]
                normed[2 * a + e, :, b * 128 : b * 128 + 128] = block
                spot = (8 * a + 4 * e + b) * 128
                plain = block.astype(F32) / gain[:, spot : spot + 128]
                squares = squares + plain * plain
    ratio = lax.rsqrt(jnp.sum(squares, axis=1, keepdims=True) / 4096 + EPSILON)

    for copy in local[1:]:
        copy.wait()
    for copy in shared[1:]:
        copy.wait_recv()
    near_ring.done()

    acc[...] = jnp.zeros(acc.shape, F32)

    def gate_up(step, carry):
        s = 2 * lax.rem(step, 4) + jnp.where(step < 4, h, far)
        for cc in range(2):
            for part in range(2):
                acc[cc, part] = acc[cc, part] + lax.dot_general(
                    normed[s],
                    gate_up_w[cc, s, part * 448 : part * 448 + 448, :],
                    nt,
                    preferred_element_type=F32,
                )
        return carry

    lax.fori_loop(0, 4, gate_up, 0)
    for p in range(4):
        far_ring.collect(p)
    for p in range(4):
        ref = gate_up_w.at[1 - k, far_s, pl.ds(p * 224, 224)]
        remote(ref, ref, core_s.at[3 + p], core_r.at[3 + p], twin).wait_recv()
    far_ring.done()
    lax.fori_loop(4, 8, gate_up, 0)
    for cc in range(2):
        gate = acc[cc, 0] * ratio
        upward = acc[cc, 1] * ratio
        inner[cc] = (gate / (1.0 + jnp.exp(-gate)) * upward).astype(BF16)

    def down(step, carry):
        zi = step // 4
        xi = step % 4
        b = up(m, zi + 1)
        a = up(x, xi + 1)
        first = pl.ds(pl.multiple_of((8 * a + b) * 128, 128), 128)
        second = pl.ds(pl.multiple_of((8 * a + 4 + b) * 128, 128), 128)
        block = jnp.zeros((192, 256), F32)
        for cc in range(2):
            weights = jnp.concatenate([down_w[cc, :, first], down_w[cc, :, second]], axis=1)
            block = block + jnp.dot(inner[cc], weights, preferred_element_type=F32)

        @pl.when(xi < 3)
        def _():
            x_out[xi, zi] = block.astype(BF16)
            remote(
                x_out.at[xi, zi], x_in.at[xi, zi], rx_s.at[xi, zi], rx_r.at[xi, zi], at_x(a)
            ).start()

        @pl.when(xi == 3)
        def _():
            x_own[zi] = block

        return carry

    lax.fori_loop(0, 16, down, 0)
    for zi in range(4):
        block = x_own[zi]
        for xi in range(3):
            remote(
                x_out.at[xi, zi], x_in.at[xi, zi], rx_s.at[xi, zi], rx_r.at[xi, zi], at_x(x_peers[xi])
            ).wait()
            block = block + x_in[xi, zi].astype(F32)
        if zi < 3:
            z_out[zi] = block.astype(BF16)
            go(remote(z_out.at[zi], z_in.at[zi], rz_s.at[zi], rz_r.at[zi], at_m(m_peers[zi])))
    block = block + resid[...]
    for zi in range(3):
        remote(z_out.at[zi], z_in.at[zi], rz_s.at[zi], rz_r.at[zi], at_m(m_peers[zi])).wait_recv()
        block = block + z_in[zi].astype(F32)
    result = block.astype(BF16)
    lower = result[:, :128]
    upper = result[:, 128:]
    swap_out[...] = jnp.where(k == 0, upper, lower)
    swap = go(remote(swap_out, swap_in, sw_s, sw_r, twin))
    kept_half = jnp.where(k == 0, lower, upper)
    for a in range(4):
        out[a, k] = kept_half[a * 48 : a * 48 + 48]
    swap.wait_recv()
    for a in range(4):
        out[a, 1 - k] = swap_in[a * 48 : a * 48 + 48, :]
    for copy in sends:
        copy.wait_send()


def rms_scale(values, gain):
    return values * lax.rsqrt(jnp.mean(values * values, axis=-1, keepdims=True) + EPSILON) * gain


def base_freq(half):
    steps = jnp.arange(half, dtype=F32)
    return jnp.exp(steps * (-2.0 * math.log(ROPE_BASE) / (2 * half)))


def per_device(
    states,
    attn_gain,
    w_query,
    w_keyval,
    kv_cache,
    page_live,
    factor_levels,
    cand_index,
    w_out,
    ffn_gain,
    w_gate_up,
    w_down,
):
    x, k, y, h, m = position()
    c = lax.axis_index("cand")
    normed = rms_scale(states.astype(F32), attn_gain).astype(BF16)
    slab = lax.dynamic_slice_in_dim(normed, c * 512, 512, 1)
    query_part = jnp.einsum("td,dkc->tkc", slab, w_query, preferred_element_type=F32)
    keyval_part = jnp.einsum("td,dkc->tkc", slab, w_keyval, preferred_element_type=F32)
    part = jnp.concatenate(
        [query_part.reshape(48, 8, 128), jnp.repeat(keyval_part.reshape(48, 4, 128), 2, axis=1)], axis=2
    ).astype(BF16)
    part = jnp.transpose(part, (1, 0, 2))
    picks = (cand_index[0][:, None] == jnp.arange(16, dtype=jnp.int32)[None, :]).astype(F32)
    factors = jnp.sum(picks * factor_levels[None, :], axis=-1)
    freq = base_freq(64) / factors
    row = jnp.arange(152, dtype=jnp.int32)
    near = (2 * y + h) * 768 + 128 * (row - 128)
    far = (2 * y + 1 - h) * 768 + 128 * (row - 134)
    where = jnp.where(row < 128, row, jnp.where(row < 134, near, jnp.where(row < 140, far, 6144 + 48 * (row - 140))))
    angle = where.astype(F32)[:, None] * jnp.concatenate([freq, freq])[None, :]
    cosines = jnp.cos(angle)
    sines = jnp.sin(angle)
    flags = jnp.pad((page_live == 1).astype(F32), (0, 122))
    flags = jnp.broadcast_to(flags[None, :], (8, 128))
    w_shard = jnp.swapaxes(w_gate_up, 1, 2).reshape(896, 512)

    vmem = pl.BlockSpec(memory_space=pltpu.VMEM)
    hbm = pl.BlockSpec(memory_space=pl.ANY)
    out = pl.pallas_call(
        layer_kernel,
        out_shape=jax.ShapeDtypeStruct((4, 2, 48, 128), BF16),
        in_specs=[vmem] * 7 + [hbm] * 3,
        out_specs=vmem,
        scratch_shapes=[
            VM((7, 48, 256), BF16),
            VM((48, 128), BF16),
            VM((48, 128), BF16),
            VM((2, 4, 4, 48, 128), BF16),
            VM((2, 4, 48, 128), BF16),
            VM((8, 96, 512), BF16),
            VM((8, 128), F32),
            VM((2, 1536, 128), BF16),
            VM((2, 1536, 128), BF16),
            VM((2, 128, 128), BF16),
            VM((2, 128, 128), BF16),
            VM((8, 1536), F32),
            VM((2, 4, 192, 128), BF16),
            VM((2, 3, 192, 128), BF16),
            VM((2, 3, 192, 128), BF16),
            VM((2, 192, 128), F32),
            VM((3, 48, 128), F32),
            VM((3, 48, 128), F32),
            VM((48, 128), F32),
            VM((4, 192, 1024), BF16),
            VM((4096, 256), BF16),
            VM((2, 8, 896, 512), BF16),
            VM((2, 448, 4096), BF16),
            VM((192, 256), F32),
            VM((4, 4, 192, 256), BF16),
            VM((8, 192, 512), BF16),
            VM((2, 2, 192, 448), F32),
            VM((2, 192, 448), BF16),
            VM((3, 4, 192, 256), BF16),
            VM((3, 4, 192, 256), BF16),
            VM((4, 192, 256), F32),
            VM((3, 192, 256), BF16),
            VM((3, 192, 256), BF16),
            VM((192, 128), BF16),
            VM((192, 128), BF16),
            DMA((7,)),
            DMA((7,)),
            DMA((15,)),
            DMA((15,)),
            DMA((8,)),
            DMA((8,)),
            DMA,
            DMA,
            DMA((3,)),
            DMA((3,)),
            DMA((4,)),
            DMA((4,)),
            DMA,
            DMA,
            DMA,
            DMA,
            DMA((2, 3)),
            DMA((2, 3)),
            DMA((3,)),
            DMA((3,)),
            DMA((4,)),
            DMA((4,)),
            DMA((2, 3, 4)),
            DMA((2, 3, 4)),
            DMA((2, 3, 4)),
            DMA((2, 3, 4)),
            DMA((7,)),
            DMA((7,)),
            DMA((3,)),
            DMA((3,)),
            DMA((4, 3)),
            DMA((4, 3)),
            DMA((3,)),
            DMA((3,)),
            DMA((4, 3)),
            DMA((4, 3)),
            DMA((3, 4)),
            DMA((3, 4)),
            DMA((3,)),
            DMA((3,)),
            DMA,
            DMA,
            DMA((3,)),
        ],
        compiler_params=pltpu.CompilerParams(
            collective_id=0, has_side_effects=True, vmem_limit_bytes=60 << 20
        ),
        name="layer",
    )(
        part,
        cosines,
        sines,
        kv_cache.reshape(768, 512),
        flags,
        states,
        ffn_gain.reshape(1, 4096),
        w_shard,
        w_out,
        w_down,
    )
    return out.reshape(8, 48, 128)


def solution(mesh):
    return jax.shard_map(
        per_device,
        mesh=mesh,
        in_specs=(
            P("ctx", None),
            P(),
            P("cand", "mp", None),
            P("cand", "mp", None),
            P("ctx", "mp", None),
            P("ctx"),
            P(),
            P("cand", None),
            P(None, ("cand", "mp")),
            P(),
            P(None, "ctx", ("cand", "mp")),
            P(("cand", "mp"), None),
        ),
        out_specs=P(None, "ctx", ("cand", "mp")),
        check_vma=False,
    )
```

```python
import functools
import math

import jax
import jax.numpy as jnp
from jax import lax
from jax.experimental import pallas as pl
from jax.experimental.pallas import tpu as pltpu
from jax.sharding import PartitionSpec as P

EPSILON = 1e-05
ROPE_BASE = 500000.0
MESH = pl.DeviceIdType.MESH
F32 = jnp.float32
BF16 = jnp.bfloat16
DMA = pltpu.SemaphoreType.DMA
VM = pltpu.VMEM


def position():
    c = lax.axis_index("cand")
    s = lax.axis_index("ctx")
    m = lax.axis_index("mp")
    return c // 2, c % 2, s // 2, s % 2, m


def dev(x, k, y, h, m):
    return {"cand": x * 2 + k, "ctx": y * 2 + h, "mp": m}


def up(value, step, size=4):
    return lax.rem(value + step, size)


def remote(src, dst, send_sem, recv_sem, target):
    return pltpu.make_async_remote_copy(
        src_ref=src,
        dst_ref=dst,
        send_sem=send_sem,
        recv_sem=recv_sem,
        device_id=target,
        device_id_type=MESH,
    )


def greet(peers, work):
    barrier = pltpu.get_barrier_semaphore()
    for peer in peers:
        pl.semaphore_signal(barrier, inc=1, device_id=peer, device_id_type=MESH)
    work()
    pl.semaphore_wait(barrier, len(peers))


def turn(values, cosine, sine):
    return values * cosine + pltpu.roll(values, 64, 1) * sine


class Ring:
    def __init__(self, go, me, at, twin, view, send_sem, recv_sem, twin_send, twin_recv):
        self.go, self.me, self.at, self.twin, self.view = go, me, at, twin, view
        self.ss, self.rs, self.ts, self.tr = send_sem, recv_sem, twin_send, twin_recv

    def copy(self, src, dst, kind, part, step):
        return remote(src, dst, self.ss.at[kind, part], self.rs.at[kind, part], self.at(up(self.me, step)))

    def send(self, part, src):
        dst = self.view(self.me, part)
        steps = (1, 3) if part % 2 == 0 else (3, 1)
        for step in steps:
            self.go(self.copy(src, dst, 0 if step == 1 else 1, part, step))

    def take(self, kind, part):
        ref = self.view(up(self.me, (3, 1, 2)[kind]), part)
        self.copy(ref, ref, kind, part, 1).wait_recv()
        self.go(remote(ref, ref, self.ts.at[kind, part], self.tr.at[kind, part], self.twin))
        return ref

    def forward(self, part):
        ref = self.take(part % 2, part)
        self.go(self.copy(ref, ref, 2, part, 1 if part % 2 == 0 else 3))

    def collect(self, part):
        self.take(1 - part % 2, part)
        self.take(2, part)

    def done(self):
        for kind in range(3):
            for part in range(4):
                ref = self.view(up(self.me, (3, 1, 2)[kind]), part)
                remote(ref, ref, self.ts.at[kind, part], self.tr.at[kind, part], self.twin).wait_recv()


def layer_kernel(
    live_pages,
    levels,
    picks,
    attn_gain,
    w_query,
    w_keyval,
    kv,
    states,
    gain,
    w_shard,
    w_out,
    w_down,
    out,
    part,
    cosines,
    sines,
    flags,
    rs_in,
    q_own,
    n_own,
    q_all,
    n_all,
    kv_far,
    flags_far,
    keys,
    vals,
    new_keys,
    new_vals,
    live,
    q_rot,
    num_out,
    num_in,
    num_own,
    den_out,
    den_in,
    den_own,
    attn_all,
    out_w,
    gate_up_w,
    down_w,
    resid,
    shards,
    normed,
    acc,
    inner,
    x_out,
    x_in,
    x_own,
    z_out,
    z_in,
    swap_out,
    swap_in,
    rs_s,
    rs_r,
    q_s,
    q_r,
    n_s,
    n_r,
    kz_s,
    kz_r,
    kf_s,
    kf_r,
    kt_s,
    kt_r,
    qt_s,
    qt_r,
    fl_s,
    fl_r,
    num_s,
    num_r,
    den_s,
    den_r,
    wz_s,
    wz_r,
    ring_s,
    ring_r,
    tw_s,
    tw_r,
    core_s,
    core_r,
    az_s,
    az_r,
    ax_s,
    ax_r,
    gz_s,
    gz_r,
    gx_s,
    gx_r,
    rx_s,
    rx_r,
    rz_s,
    rz_r,
    sw_s,
    sw_r,
    loc,
):
    x, k, y, h, m = position()
    c = x * 2 + k
    far = 1 - h
    cand_peers = [(x, 1 - k)] + [(up(x, i), kk) for i in (1, 2, 3) for kk in (k, 1 - k)]
    xy_peers = [(up(x, i), up(y, j)) for j in range(4) for i in range(4) if i or j]
    zhi = dev(x, k, y, far, m)
    x_peers = [up(x, i) for i in (1, 2, 3)]
    m_peers = [up(m, i) for i in (1, 2, 3)]
    twin = dev(x, 1 - k, y, h, m)
    near_s = 2 * y + h
    far_s = 2 * y + far

    def at_x(a):
        return dev(a, k, y, h, m)

    def at_y(a):
        return dev(x, k, a, h, m)

    def at_m(a):
        return dev(x, k, y, h, a)

    def prepare():
        values = states[...].astype(F32)
        ratio = lax.rsqrt(jnp.sum(values * values, axis=1, keepdims=True) / 4096 + EPSILON)
        slab = pl.ds(pl.multiple_of(c * 512, 512), 512)
        normed_slab = (states[:, slab].astype(F32) * ratio * attn_gain[:, slab]).astype(BF16)
        queries = jnp.dot(normed_slab, w_query[...], preferred_element_type=F32).astype(BF16)
        keyvals = jnp.dot(normed_slab, w_keyval[...], preferred_element_type=F32).astype(BF16)
        for head in range(8):
            part[head, :, :128] = queries[:, head * 128 : head * 128 + 128]
            spot = head // 2 * 128
            part[head, :, 128:] = keyvals[:, spot : spot + 128]
        page_lane = lax.broadcasted_iota(jnp.int32, (8, 128), 1)
        marks = jnp.zeros((8, 128), F32)
        for page in range(6):
            marks = jnp.where(page_lane == page, live_pages[page].astype(F32), marks)
        flags[...] = marks

    def make_tables():
        pick = jnp.concatenate([picks[...], picks[...]], axis=1)
        factor = jnp.zeros((1, 128), F32)
        for level in range(16):
            factor = jnp.where(pick == level, levels[level], factor)
        lane = lax.broadcasted_iota(jnp.int32, (1, 128), 1)
        step = jnp.where(lane < 64, lane, lane - 64).astype(F32)
        freq = jnp.exp(step * (-2.0 * math.log(ROPE_BASE) / 128)) / factor
        row = lax.broadcasted_iota(jnp.int32, (152, 128), 0)
        near = near_s * 768 + 128 * (row - 128)
        other = far_s * 768 + 128 * (row - 134)
        where = jnp.where(
            row < 128, row, jnp.where(row < 134, near, jnp.where(row < 140, other, 6144 + 48 * (row - 140)))
        )
        angle = where.astype(F32) * freq
        cosines[...] = jnp.cos(angle)
        sines[...] = jnp.sin(angle)

    greet(
        [dev(a, b, y, h, m) for a, b in cand_peers]
        + [dev(a, k, b, h, m) for a, b in xy_peers[3:]]
        + [dev(up(x, i), k, y, far, m) for i in range(4)]
        + [at_m(a) for a in m_peers],
        prepare,
    )
    rows = kv_far.shape[1]
    sends = []

    def go(copy):
        copy.start()
        sends.append(copy)
        return copy

    for i, (a, b) in enumerate(cand_peers):
        go(remote(part.at[2 * a + b], rs_in.at[i], rs_s.at[i], rs_r.at[i], dev(a, b, y, h, m)))
    mine = kv.at[pl.ds(pl.multiple_of(c * rows, 16), rows)]
    kz = go(remote(mine, kv_far.at[c], kz_s, kz_r, zhi))
    fl = go(remote(flags, flags_far, fl_s, fl_r, zhi))
    side = pl.ds(pl.multiple_of(k * 128, 128), 128)
    pairs = [
        (w_out, out_w.at[:, side]),
        (w_shard, gate_up_w.at[k, near_s]),
        (w_down, down_w.at[k]),
    ]
    local = []
    shared = []
    for i, (src, dst) in enumerate(pairs):
        copy = pltpu.make_async_copy(src, dst, loc.at[i])
        copy.start()
        local.append(copy)
        shared.append(go(remote(src, dst, core_s.at[i], core_r.at[i], twin)))

    def near_view(b, part):
        return gate_up_w.at[k, 2 * b + h, pl.ds(part * 224, 224)]

    def far_view(b, part):
        return gate_up_w.at[k, 2 * b + far, pl.ds(part * 224, 224)]

    near_ring = Ring(go, y, at_y, twin, near_view, ring_s.at[0], ring_r.at[0], tw_s.at[0], tw_r.at[0])
    far_ring = Ring(go, y, at_y, twin, far_view, ring_s.at[1], ring_r.at[1], tw_s.at[1], tw_r.at[1])

    def send_near(p):
        near_ring.send(p, w_shard.at[pl.ds(p * 224, 224)])

    def send_far(p):
        go(remote(w_shard.at[pl.ds(p * 224, 224)], near_view(y, p), wz_s.at[p], wz_r.at[p], zhi))

    def take_far(p):
        ref = far_view(y, p)
        remote(ref, ref, wz_s.at[p], wz_r.at[p], zhi).wait_recv()
        go(remote(ref, ref, core_s.at[3 + p], core_r.at[3 + p], twin))
        far_ring.send(p, ref)

    for p in (0,):
        send_near(p)
    send_near(1)
    half = kv.shape[0]

    make_tables()
    sign = jnp.where(lax.broadcasted_iota(jnp.int32, (1, 128), 1) < 64, -1.0, 1.0)

    def angles(base, count):
        first_cos = cosines[pl.ds(base, 1), :]
        first_sin = sines[pl.ds(base, 1), :]
        place_cos = cosines[pl.ds(0, count), :]
        place_sin = sines[pl.ds(0, count), :]
        return (
            first_cos * place_cos - first_sin * place_sin,
            (first_sin * place_cos + first_cos * place_sin) * sign,
        )

    def place_page(side, page, source):
        cosine, sine = angles(128 + side * 6 + page, 128)
        rows = pl.ds(side * half + page * 128, 128)
        for j in range(2):
            raw = source[:, j * 256 : j * 256 + 128].astype(F32)
            keys[j, rows, :] = turn(raw, cosine, sine).astype(BF16)
            vals[j, rows, :] = source[:, j * 256 + 128 : j * 256 + 256]

    for page in range(6):
        place_page(0, page, kv[page * 128 : page * 128 + 128, :])
    for j in range(2):
        new_keys[j] = jnp.zeros(new_keys.shape[1:], BF16)
        new_vals[j] = jnp.zeros(new_vals.shape[1:], BF16)

    for i, (a, b) in enumerate(cand_peers):
        remote(part.at[c], rs_in.at[i], rs_s.at[i], rs_r.at[i], dev(a, b, y, h, m)).wait_recv()
    total = part[c].astype(F32)
    for i in range(7):
        total = total + rs_in[i].astype(F32)
    summed = total.astype(BF16)
    q_own[...] = summed[:, :128]
    n_own[...] = summed[:, 128:]
    q_all[k, y, x] = summed[:, :128]
    n_all[0, x] = summed[:, 128:]
    for i, (a, b) in enumerate(xy_peers):
        go(remote(q_own, q_all.at[k, y, x], q_s.at[i], q_r.at[i], dev(a, k, b, h, m)))
    for i in (1, 2, 3):
        go(remote(n_own, n_all.at[0, x], n_s.at[i], n_r.at[i], dev(up(x, i), k, y, h, m)))
    for i in range(4):
        go(remote(n_own, n_all.at[1, x], n_s.at[4 + i], n_r.at[4 + i], dev(up(x, i), k, y, far, m)))

    for p in (0, 1):
        send_far(p)
    for p in (2, 3):
        send_near(p)
    kz.wait_recv()
    for i, a in enumerate(x_peers):
        go(remote(kv_far.at[c], kv_far.at[c], kf_s.at[i], kf_r.at[i], at_x(a)))
    go(remote(kv_far.at[c], kv_far.at[c], kt_s.at[3], kt_r.at[3], twin))
    fl.wait_recv()
    for page in range(6):
        live[:, page * 128 : page * 128 + 128] = jnp.broadcast_to(flags[:, page : page + 1], (8, 128))
        live[:, half + page * 128 : half + page * 128 + 128] = jnp.broadcast_to(
            flags_far[:, page : page + 1], (8, 128)
        )

    for i, (a, b) in enumerate(xy_peers):
        remote(q_own, q_all.at[k, b, a], q_s.at[i], q_r.at[i], dev(a, k, b, h, m)).wait_recv()
    pair = go(remote(q_all.at[k], q_all.at[k], qt_s, qt_r, twin))
    for i in (1, 2, 3):
        remote(n_own, n_all.at[0, x], n_s.at[i], n_r.at[i], zhi).wait_recv()
    for i in range(4):
        remote(n_own, n_all.at[1, x], n_s.at[4 + i], n_r.at[4 + i], zhi).wait_recv()
    for block in range(2):
        cosine, sine = angles(140 + 2 * y + (h if block == 0 else far), 48)
        for j in range(2):
            raw = n_all[block, 2 * j].astype(F32)
            spot = block * 48
            new_keys[j, spot : spot + 48, :] = turn(raw, cosine, sine).astype(BF16)
            new_vals[j, spot : spot + 48, :] = n_all[block, 2 * j + 1]
    pair.wait_recv()

    def turn_queries(b, carry):
        cosine, sine = angles(140 + 2 * b + h, 48)
        for head in range(8):
            raw = q_all[head % 2, b, head // 2].astype(F32)
            spot = (head % 4) * 48
            q_rot[head // 4, b, spot : spot + 48, :] = turn(raw, cosine, sine).astype(BF16)
        return carry

    lax.fori_loop(0, 4, turn_queries, 0)

    for i in range(3):
        came = kv_far.at[2 * up(x, 3 - i) + k]
        remote(came, came, kf_s.at[i], kf_r.at[i], twin).wait_recv()
        go(remote(came, came, kt_s.at[i], kt_r.at[i], twin))
    for i in range(4):
        came = kv_far.at[2 * up(x, 3 - i) + 1 - k]
        remote(came, came, kt_s.at[i], kt_r.at[i], twin).wait_recv()
    far_rows = kv_far[...].reshape(half, kv.shape[1])
    for page in range(6):
        place_page(1, page, far_rows[page * 128 : page * 128 + 128])

    scale = 128 ** (-0.5)
    lane = lax.broadcasted_iota(jnp.int32, (48, 128), 1)
    key_lane = lax.broadcasted_iota(jnp.int32, (192, 128), 1)
    token = lax.broadcasted_iota(jnp.int32, (4, 48, 128), 1).reshape(192, 128)
    first = (2 * y + h) * 48
    second = (2 * y + far) * 48
    key_index = jnp.where(
        key_lane < 48, first + key_lane, jnp.where(key_lane < 96, second + key_lane - 48, 1 << 20)
    )
    nt = (((1,), (1,)), ((), ()))

    def attend(step, carry):
        j = step // 4
        i = step % 4
        b = up(y, i + 1)
        query = q_rot[j, b]
        scores = lax.dot_general(query, keys[j], nt, preferred_element_type=F32)
        expo = jnp.where(live[0:1, :] > 0.5, jnp.exp(scores * scale), 0.0)
        recent = lax.dot_general(query, new_keys[j], nt, preferred_element_type=F32)
        seen = key_index <= (2 * b + h) * 48 + token
        recent_expo = jnp.where(seen, jnp.exp(recent * scale), 0.0)
        denom = jnp.sum(expo, axis=1, keepdims=True) + jnp.sum(recent_expo, axis=1, keepdims=True)
        numer = jnp.dot(expo.astype(BF16), vals[j], preferred_element_type=F32)
        numer = numer + jnp.dot(recent_expo.astype(BF16), new_vals[j], preferred_element_type=F32)
        lanes = jnp.zeros((48, 128), F32)
        for g in range(4):
            lanes = lanes + jnp.where(lane == j * 4 + g, denom[g * 48 : g * 48 + 48], 0.0)

        @pl.when(i < 3)
        def _():
            num_out[j, i] = numer.astype(BF16)
            remote(
                num_out.at[j, i], num_in.at[j, i], num_s.at[j, i], num_r.at[j, i], dev(x, k, b, h, m)
            ).start()

            @pl.when(j == 0)
            def _():
                den_out[i] = lanes

            @pl.when(j == 1)
            def _():
                den_out[i] = den_out[i] + lanes
                remote(
                    den_out.at[i], den_in.at[i], den_s.at[i], den_r.at[i], dev(x, k, b, h, m)
                ).start()

        @pl.when(i == 3)
        def _():
            num_own[j] = numer

            @pl.when(j == 0)
            def _():
                den_own[...] = lanes

            @pl.when(j == 1)
            def _():
                den_own[...] = den_own[...] + lanes

        return carry

    lax.fori_loop(0, 8, attend, 0)
    send_far(2)
    for p in range(4):
        near_ring.forward(p)
    for p in (0, 1):
        take_far(p)

    denom = den_own[...]
    for i in range(3):
        copy = remote(den_out.at[i], den_in.at[i], den_s.at[i], den_r.at[i], dev(x, k, up(y, i + 1), h, m))
        copy.wait()
        denom = denom + den_in[i]
    for j in range(2):
        numer = num_own[j]
        for i in range(3):
            remote(
                num_out.at[j, i],
                num_in.at[j, i],
                num_s.at[j, i],
                num_r.at[j, i],
                dev(x, k, up(y, i + 1), h, m),
            ).wait()
            numer = numer + num_in[j, i].astype(F32)
        for g in range(4):
            head = j * 4 + g
            attn_all[m, pl.ds(pl.multiple_of(x * 48, 16), 48), head * 128 : head * 128 + 128] = (
                numer[g * 48 : g * 48 + 48] / denom[:, head : head + 1]
            ).astype(BF16)


    def gather(view, zs, zr, xs, xr):
        own = view(x, m)
        for i, b in enumerate(m_peers):
            go(remote(own, own, zs.at[i], zr.at[i], at_m(b)))
        for j, a in enumerate(x_peers):
            go(remote(own, own, xs.at[3, j], xr.at[3, j], at_x(a)))
        for i in range(3):
            came = view(x, up(m, 3 - i))
            remote(own, came, zs.at[i], zr.at[i], at_m(m_peers[i])).wait_recv()
            for j, a in enumerate(x_peers):
                go(remote(came, came, xs.at[i, j], xr.at[i, j], at_x(a)))

    def gather_rest(view, xs, xr):
        for i in (3, 0, 1, 2):
            for j in range(3):
                came = view(up(x, 3 - j), up(m, 3 - i) if i < 3 else m)
                remote(came, came, xs.at[i, j], xr.at[i, j], at_x(x_peers[j])).wait_recv()

    def attn_view(a, b):
        return attn_all.at[b, pl.ds(pl.multiple_of(a * 48, 16), 48)]

    gather(attn_view, az_s, az_r, ax_s, ax_r)
    send_far(3)
    for p in range(4):
        near_ring.collect(p)
    take_far(2)
    for p in (0, 1):
        far_ring.forward(p)
    gather_rest(attn_view, ax_s, ax_r)
    local[0].wait()
    shared[0].wait_recv()

    total = jnp.dot(attn_all[0], out_w[0:1024, :], preferred_element_type=F32)
    for b in range(1, 4):
        total = total + jnp.dot(
            attn_all[b], out_w[b * 1024 : b * 1024 + 1024, :], preferred_element_type=F32
        )
    even = pl.ds(pl.multiple_of((8 * x + m) * 128, 128), 128)
    odd = pl.ds(pl.multiple_of((8 * x + 4 + m) * 128, 128), 128)
    columns = jnp.concatenate([states[:, even], states[:, odd]], axis=1).astype(F32)
    gains = jnp.concatenate([gain[:, even], gain[:, odd]], axis=1)
    kept = total + jnp.concatenate([columns] * 4, axis=0)
    resid[...] = kept

    def shard_view(a, b):
        return shards.at[a, b]

    shards[x, m] = (kept * gains).astype(BF16)
    gather(shard_view, gz_s, gz_r, gx_s, gx_r)

    take_far(3)
    far_ring.forward(2)
    gather_rest(shard_view, gx_s, gx_r)
    far_ring.forward(3)

    squares = jnp.zeros((192, 128), F32)
    for a in range(4):
        for b in range(4):
            for e in range(2):
                block = shards[a, b, :, e * 128 : e * 128 + 128]
                normed[2 * a + e, :, b * 128 : b * 128 + 128] = block
                spot = (8 * a + 4 * e + b) * 128
                plain = block.astype(F32) / gain[:, spot : spot + 128]
                squares = squares + plain * plain
    ratio = lax.rsqrt(jnp.sum(squares, axis=1, keepdims=True) / 4096 + EPSILON)

    for copy in local[1:]:
        copy.wait()
    for copy in shared[1:]:
        copy.wait_recv()
    near_ring.done()

    acc[...] = jnp.zeros(acc.shape, F32)

    def gate_up(step, carry):
        s = 2 * lax.rem(step, 4) + jnp.where(step < 4, h, far)
        for cc in range(2):
            for part in range(2):
                acc[cc, part] = acc[cc, part] + lax.dot_general(
                    normed[s],
                    gate_up_w[cc, s, part * 448 : part * 448 + 448, :],
                    nt,
                    preferred_element_type=F32,
                )
        return carry

    lax.fori_loop(0, 4, gate_up, 0)
    for p in range(4):
        far_ring.collect(p)
    for p in range(4):
        ref = gate_up_w.at[1 - k, far_s, pl.ds(p * 224, 224)]
        remote(ref, ref, core_s.at[3 + p], core_r.at[3 + p], twin).wait_recv()
    far_ring.done()
    lax.fori_loop(4, 8, gate_up, 0)
    for cc in range(2):
        gate = acc[cc, 0] * ratio
        upward = acc[cc, 1] * ratio
        inner[cc] = (gate / (1.0 + jnp.exp(-gate)) * upward).astype(BF16)

    def down(step, carry):
        zi = step // 4
        xi = step % 4
        b = up(m, zi + 1)
        a = up(x, xi + 1)
        first = pl.ds(pl.multiple_of((8 * a + b) * 128, 128), 128)
        second = pl.ds(pl.multiple_of((8 * a + 4 + b) * 128, 128), 128)
        block = jnp.zeros((192, 256), F32)
        for cc in range(2):
            weights = jnp.concatenate([down_w[cc, :, first], down_w[cc, :, second]], axis=1)
            block = block + jnp.dot(inner[cc], weights, preferred_element_type=F32)

        @pl.when(xi < 3)
        def _():
            x_out[xi, zi] = block.astype(BF16)
            remote(
                x_out.at[xi, zi], x_in.at[xi, zi], rx_s.at[xi, zi], rx_r.at[xi, zi], at_x(a)
            ).start()

        @pl.when(xi == 3)
        def _():
            x_own[zi] = block

        return carry

    lax.fori_loop(0, 16, down, 0)
    for zi in range(4):
        block = x_own[zi]
        for xi in range(3):
            remote(
                x_out.at[xi, zi], x_in.at[xi, zi], rx_s.at[xi, zi], rx_r.at[xi, zi], at_x(x_peers[xi])
            ).wait()
            block = block + x_in[xi, zi].astype(F32)
        if zi < 3:
            z_out[zi] = block.astype(BF16)
            go(remote(z_out.at[zi], z_in.at[zi], rz_s.at[zi], rz_r.at[zi], at_m(m_peers[zi])))
    block = block + resid[...]
    for zi in range(3):
        remote(z_out.at[zi], z_in.at[zi], rz_s.at[zi], rz_r.at[zi], at_m(m_peers[zi])).wait_recv()
        block = block + z_in[zi].astype(F32)
    result = block.astype(BF16)
    lower = result[:, :128]
    upper = result[:, 128:]
    swap_out[...] = jnp.where(k == 0, upper, lower)
    swap = go(remote(swap_out, swap_in, sw_s, sw_r, twin))
    kept_half = jnp.where(k == 0, lower, upper)
    for a in range(4):
        out[a, k] = kept_half[a * 48 : a * 48 + 48]
    swap.wait_recv()
    for a in range(4):
        out[a, 1 - k] = swap_in[a * 48 : a * 48 + 48, :]
    for copy in sends:
        copy.wait_send()


def per_device(
    states,
    attn_gain,
    w_query,
    w_keyval,
    kv_cache,
    page_live,
    factor_levels,
    cand_index,
    w_out,
    ffn_gain,
    w_gate_up,
    w_down,
):
    w_shard = jnp.swapaxes(w_gate_up, 1, 2).reshape(896, 512)

    vmem = pl.BlockSpec(memory_space=pltpu.VMEM)
    hbm = pl.BlockSpec(memory_space=pl.ANY)
    smem = pl.BlockSpec(memory_space=pltpu.SMEM)
    out = pl.pallas_call(
        layer_kernel,
        out_shape=jax.ShapeDtypeStruct((4, 2, 48, 128), BF16),
        in_specs=[smem] * 2 + [vmem] * 7 + [hbm] * 3,
        out_specs=vmem,
        scratch_shapes=[
            VM((8, 48, 256), BF16),
            VM((152, 128), F32),
            VM((152, 128), F32),
            VM((8, 128), F32),
            VM((7, 48, 256), BF16),
            VM((48, 128), BF16),
            VM((48, 128), BF16),
            VM((2, 4, 4, 48, 128), BF16),
            VM((2, 4, 48, 128), BF16),
            VM((8, 96, 512), BF16),
            VM((8, 128), F32),
            VM((2, 1536, 128), BF16),
            VM((2, 1536, 128), BF16),
            VM((2, 128, 128), BF16),
            VM((2, 128, 128), BF16),
            VM((8, 1536), F32),
            VM((2, 4, 192, 128), BF16),
            VM((2, 3, 192, 128), BF16),
            VM((2, 3, 192, 128), BF16),
            VM((2, 192, 128), F32),
            VM((3, 48, 128), F32),
            VM((3, 48, 128), F32),
            VM((48, 128), F32),
            VM((4, 192, 1024), BF16),
            VM((4096, 256), BF16),
            VM((2, 8, 896, 512), BF16),
            VM((2, 448, 4096), BF16),
            VM((192, 256), F32),
            VM((4, 4, 192, 256), BF16),
            VM((8, 192, 512), BF16),
            VM((2, 2, 192, 448), F32),
            VM((2, 192, 448), BF16),
            VM((3, 4, 192, 256), BF16),
            VM((3, 4, 192, 256), BF16),
            VM((4, 192, 256), F32),
            VM((3, 192, 256), BF16),
            VM((3, 192, 256), BF16),
            VM((192, 128), BF16),
            VM((192, 128), BF16),
            DMA((7,)),
            DMA((7,)),
            DMA((15,)),
            DMA((15,)),
            DMA((8,)),
            DMA((8,)),
            DMA,
            DMA,
            DMA((3,)),
            DMA((3,)),
            DMA((4,)),
            DMA((4,)),
            DMA,
            DMA,
            DMA,
            DMA,
            DMA((2, 3)),
            DMA((2, 3)),
            DMA((3,)),
            DMA((3,)),
            DMA((4,)),
            DMA((4,)),
            DMA((2, 3, 4)),
            DMA((2, 3, 4)),
            DMA((2, 3, 4)),
            DMA((2, 3, 4)),
            DMA((7,)),
            DMA((7,)),
            DMA((3,)),
            DMA((3,)),
            DMA((4, 3)),
            DMA((4, 3)),
            DMA((3,)),
            DMA((3,)),
            DMA((4, 3)),
            DMA((4, 3)),
            DMA((3, 4)),
            DMA((3, 4)),
            DMA((3,)),
            DMA((3,)),
            DMA,
            DMA,
            DMA((3,)),
        ],
        compiler_params=pltpu.CompilerParams(
            collective_id=0, has_side_effects=True, vmem_limit_bytes=60 << 20
        ),
        name="layer",
    )(
        page_live,
        factor_levels,
        cand_index,
        attn_gain.reshape(1, 4096),
        w_query.reshape(512, 1024),
        w_keyval.reshape(512, 512),
        kv_cache.reshape(768, 512),
        states,
        ffn_gain.reshape(1, 4096),
        w_shard,
        w_out,
        w_down,
    )
    return out.reshape(8, 48, 128)


def solution(mesh):
    return jax.shard_map(
        per_device,
        mesh=mesh,
        in_specs=(
            P("ctx", None),
            P(),
            P("cand", "mp", None),
            P("cand", "mp", None),
            P("ctx", "mp", None),
            P("ctx"),
            P(),
            P("cand", None),
            P(None, ("cand", "mp")),
            P(),
            P(None, "ctx", ("cand", "mp")),
            P(("cand", "mp"), None),
        ),
        out_specs=P(None, "ctx", ("cand", "mp")),
        check_vma=False,
    )
```

```python
import functools
import math

import jax
import jax.numpy as jnp
from jax import lax
from jax.experimental import pallas as pl
from jax.experimental.pallas import tpu as pltpu
from jax.sharding import PartitionSpec as P

EPSILON = 1e-05
ROPE_BASE = 500000.0
MESH = pl.DeviceIdType.MESH
F32 = jnp.float32
BF16 = jnp.bfloat16
DMA = pltpu.SemaphoreType.DMA
VM = pltpu.VMEM


def position():
    c = lax.axis_index("cand")
    s = lax.axis_index("ctx")
    m = lax.axis_index("mp")
    return c // 2, c % 2, s // 2, s % 2, m


def dev(x, k, y, h, m):
    return {"cand": x * 2 + k, "ctx": y * 2 + h, "mp": m}


def up(value, step, size=4):
    return lax.rem(value + step, size)


def remote(src, dst, send_sem, recv_sem, target):
    return pltpu.make_async_remote_copy(
        src_ref=src,
        dst_ref=dst,
        send_sem=send_sem,
        recv_sem=recv_sem,
        device_id=target,
        device_id_type=MESH,
    )


def greet(peers, work):
    barrier = pltpu.get_barrier_semaphore()
    for peer in peers:
        pl.semaphore_signal(barrier, inc=1, device_id=peer, device_id_type=MESH)
    work()
    pl.semaphore_wait(barrier, len(peers))


def turn(values, cosine, sine):
    return values * cosine + pltpu.roll(values, 64, 1) * sine


class Ring:
    def __init__(self, go, me, at, twin, view, send_sem, recv_sem, twin_send, twin_recv):
        self.go, self.me, self.at, self.twin, self.view = go, me, at, twin, view
        self.ss, self.rs, self.ts, self.tr = send_sem, recv_sem, twin_send, twin_recv

    def copy(self, src, dst, kind, part, step):
        return remote(src, dst, self.ss.at[kind, part], self.rs.at[kind, part], self.at(up(self.me, step)))

    def send(self, part, src):
        dst = self.view(self.me, part)
        steps = (1, 3) if part % 2 == 0 else (3, 1)
        for step in steps:
            self.go(self.copy(src, dst, 0 if step == 1 else 1, part, step))

    def take(self, kind, part):
        ref = self.view(up(self.me, (3, 1, 2)[kind]), part)
        self.copy(ref, ref, kind, part, 1).wait_recv()
        self.go(remote(ref, ref, self.ts.at[kind, part], self.tr.at[kind, part], self.twin))
        return ref

    def forward(self, part):
        ref = self.take(part % 2, part)
        self.go(self.copy(ref, ref, 2, part, 1 if part % 2 == 0 else 3))

    def collect(self, part):
        self.take(1 - part % 2, part)
        self.take(2, part)

    def done(self):
        for kind in range(3):
            for part in range(4):
                ref = self.view(up(self.me, (3, 1, 2)[kind]), part)
                remote(ref, ref, self.ts.at[kind, part], self.tr.at[kind, part], self.twin).wait_recv()


def layer_kernel(
    live_pages,
    levels,
    picks,
    attn_gain,
    w_query,
    w_keyval,
    kv,
    states,
    gain,
    w_shard,
    w_out,
    w_down,
    out,
    part,
    cosines,
    sines,
    flags,
    rs_in,
    q_own,
    n_own,
    q_all,
    n_all,
    kv_far,
    flags_far,
    keys,
    vals,
    new_keys,
    new_vals,
    live,
    q_rot,
    num_out,
    num_in,
    num_own,
    den_out,
    den_in,
    den_own,
    attn_all,
    out_w,
    gate_up_w,
    down_w,
    resid,
    shards,
    normed,
    acc,
    inner,
    x_out,
    x_in,
    x_own,
    z_out,
    z_in,
    swap_out,
    swap_in,
    rs_s,
    rs_r,
    q_s,
    q_r,
    n_s,
    n_r,
    kz_s,
    kz_r,
    kf_s,
    kf_r,
    kt_s,
    kt_r,
    qt_s,
    qt_r,
    fl_s,
    fl_r,
    num_s,
    num_r,
    den_s,
    den_r,
    wz_s,
    wz_r,
    ring_s,
    ring_r,
    tw_s,
    tw_r,
    core_s,
    core_r,
    az_s,
    az_r,
    ax_s,
    ax_r,
    gz_s,
    gz_r,
    gx_s,
    gx_r,
    rx_s,
    rx_r,
    rz_s,
    rz_r,
    sw_s,
    sw_r,
    loc,
):
    x, k, y, h, m = position()
    c = x * 2 + k
    far = 1 - h
    cand_peers = [(x, 1 - k)] + [(up(x, i), kk) for i in (1, 2, 3) for kk in (k, 1 - k)]
    xy_peers = [(up(x, i), up(y, j)) for j in range(4) for i in range(4) if i or j]
    zhi = dev(x, k, y, far, m)
    x_peers = [up(x, i) for i in (1, 2, 3)]
    m_peers = [up(m, i) for i in (1, 2, 3)]
    twin = dev(x, 1 - k, y, h, m)
    near_s = 2 * y + h
    far_s = 2 * y + far

    def at_x(a):
        return dev(a, k, y, h, m)

    def at_y(a):
        return dev(x, k, a, h, m)

    def at_m(a):
        return dev(x, k, y, h, a)

    def prepare():
        values = states[...].astype(F32)
        ratio = lax.rsqrt(jnp.sum(values * values, axis=1, keepdims=True) / 4096 + EPSILON)
        slab = pl.ds(pl.multiple_of(c * 512, 512), 512)
        normed_slab = (states[:, slab].astype(F32) * ratio * attn_gain[:, slab]).astype(BF16)
        for j in range(2):
            queries = jnp.dot(normed_slab, w_query[:, j, :], preferred_element_type=F32).astype(BF16)
            keyvals = jnp.dot(normed_slab, w_keyval[:, j, :], preferred_element_type=F32).astype(BF16)
            for g in range(4):
                part[4 * j + g, :, :128] = queries[:, g * 128 : g * 128 + 128]
                spot = g // 2 * 128
                part[4 * j + g, :, 128:] = keyvals[:, spot : spot + 128]

    def mark_pages():
        page_lane = lax.broadcasted_iota(jnp.int32, (8, 128), 1)
        marks = jnp.zeros((8, 128), F32)
        for page in range(6):
            marks = jnp.where(page_lane == page, live_pages[page].astype(F32), marks)
        flags[...] = marks

    def make_tables():
        pick = jnp.concatenate([picks[...], picks[...]], axis=1)
        factor = jnp.zeros((1, 128), F32)
        for level in range(16):
            factor = jnp.where(pick == level, levels[level], factor)
        lane = lax.broadcasted_iota(jnp.int32, (1, 128), 1)
        step = jnp.where(lane < 64, lane, lane - 64).astype(F32)
        freq = jnp.exp(step * (-2.0 * math.log(ROPE_BASE) / 128)) / factor
        row = lax.broadcasted_iota(jnp.int32, (152, 128), 0)
        near = near_s * 768 + 128 * (row - 128)
        other = far_s * 768 + 128 * (row - 134)
        where = jnp.where(
            row < 128, row, jnp.where(row < 134, near, jnp.where(row < 140, other, 6144 + 48 * (row - 140)))
        )
        angle = where.astype(F32) * freq
        cosines[...] = jnp.cos(angle)
        sines[...] = jnp.sin(angle)

    greet(
        [dev(a, b, y, h, m) for a, b in cand_peers]
        + [dev(a, k, b, h, m) for a, b in xy_peers[3:]]
        + [dev(up(x, i), k, y, far, m) for i in range(4)]
        + [at_m(a) for a in m_peers],
        mark_pages,
    )
    rows = kv_far.shape[1]
    sends = []

    def go(copy):
        copy.start()
        sends.append(copy)
        return copy

    mine = kv.at[pl.ds(pl.multiple_of(c * rows, 16), rows)]
    kz = go(remote(mine, kv_far.at[c], kz_s, kz_r, zhi))
    fl = go(remote(flags, flags_far, fl_s, fl_r, zhi))
    side = pl.ds(pl.multiple_of(k * 128, 128), 128)
    pairs = [
        (w_out, out_w.at[:, side]),
        (w_shard, gate_up_w.at[k, near_s]),
        (w_down, down_w.at[k]),
    ]
    local = []
    shared = []
    for i, (src, dst) in enumerate(pairs):
        copy = pltpu.make_async_copy(src, dst, loc.at[i])
        copy.start()
        local.append(copy)
        shared.append(go(remote(src, dst, core_s.at[i], core_r.at[i], twin)))

    def near_view(b, part):
        return gate_up_w.at[k, 2 * b + h, pl.ds(part * 224, 224)]

    def far_view(b, part):
        return gate_up_w.at[k, 2 * b + far, pl.ds(part * 224, 224)]

    near_ring = Ring(go, y, at_y, twin, near_view, ring_s.at[0], ring_r.at[0], tw_s.at[0], tw_r.at[0])
    far_ring = Ring(go, y, at_y, twin, far_view, ring_s.at[1], ring_r.at[1], tw_s.at[1], tw_r.at[1])

    def send_near(p):
        near_ring.send(p, w_shard.at[pl.ds(p * 224, 224)])

    def send_far(p):
        go(remote(w_shard.at[pl.ds(p * 224, 224)], near_view(y, p), wz_s.at[p], wz_r.at[p], zhi))

    def take_far(p):
        ref = far_view(y, p)
        remote(ref, ref, wz_s.at[p], wz_r.at[p], zhi).wait_recv()
        go(remote(ref, ref, core_s.at[3 + p], core_r.at[3 + p], twin))
        far_ring.send(p, ref)

    for p in (0,):
        send_near(p)
    send_near(1)
    prepare()
    for i, (a, b) in enumerate(cand_peers):
        go(remote(part.at[2 * a + b], rs_in.at[i], rs_s.at[i], rs_r.at[i], dev(a, b, y, h, m)))
    half = kv.shape[0]

    make_tables()
    sign = jnp.where(lax.broadcasted_iota(jnp.int32, (1, 128), 1) < 64, -1.0, 1.0)

    def angles(base, count):
        first_cos = cosines[pl.ds(base, 1), :]
        first_sin = sines[pl.ds(base, 1), :]
        place_cos = cosines[pl.ds(0, count), :]
        place_sin = sines[pl.ds(0, count), :]
        return (
            first_cos * place_cos - first_sin * place_sin,
            (first_sin * place_cos + first_cos * place_sin) * sign,
        )

    def place_page(side, page, source):
        cosine, sine = angles(128 + side * 6 + page, 128)
        rows = pl.ds(side * half + page * 128, 128)
        for j in range(2):
            raw = source[:, j, :128].astype(F32)
            keys[j, rows, :] = turn(raw, cosine, sine).astype(BF16)
            vals[j, rows, :] = source[:, j, 128:]

    for page in range(6):
        place_page(0, page, kv[page * 128 : page * 128 + 128])
    for j in range(2):
        new_keys[j] = jnp.zeros(new_keys.shape[1:], BF16)
        new_vals[j] = jnp.zeros(new_vals.shape[1:], BF16)

    for i, (a, b) in enumerate(cand_peers):
        remote(part.at[c], rs_in.at[i], rs_s.at[i], rs_r.at[i], dev(a, b, y, h, m)).wait_recv()
    total = part[c].astype(F32)
    for i in range(7):
        total = total + rs_in[i].astype(F32)
    summed = total.astype(BF16)
    q_own[...] = summed[:, :128]
    n_own[...] = summed[:, 128:]
    q_all[k, y, x] = summed[:, :128]
    n_all[0, x] = summed[:, 128:]
    for i, (a, b) in enumerate(xy_peers):
        go(remote(q_own, q_all.at[k, y, x], q_s.at[i], q_r.at[i], dev(a, k, b, h, m)))
    for i in (1, 2, 3):
        go(remote(n_own, n_all.at[0, x], n_s.at[i], n_r.at[i], dev(up(x, i), k, y, h, m)))
    for i in range(4):
        go(remote(n_own, n_all.at[1, x], n_s.at[4 + i], n_r.at[4 + i], dev(up(x, i), k, y, far, m)))

    for p in (0, 1):
        send_far(p)
    for p in (2, 3):
        send_near(p)
    kz.wait_recv()
    for i, a in enumerate(x_peers):
        go(remote(kv_far.at[c], kv_far.at[c], kf_s.at[i], kf_r.at[i], at_x(a)))
    go(remote(kv_far.at[c], kv_far.at[c], kt_s.at[3], kt_r.at[3], twin))
    fl.wait_recv()
    for page in range(6):
        live[:, page * 128 : page * 128 + 128] = jnp.broadcast_to(flags[:, page : page + 1], (8, 128))
        live[:, half + page * 128 : half + page * 128 + 128] = jnp.broadcast_to(
            flags_far[:, page : page + 1], (8, 128)
        )

    for i, (a, b) in enumerate(xy_peers):
        remote(q_own, q_all.at[k, b, a], q_s.at[i], q_r.at[i], dev(a, k, b, h, m)).wait_recv()
    pair = go(remote(q_all.at[k], q_all.at[k], qt_s, qt_r, twin))
    for i in (1, 2, 3):
        remote(n_own, n_all.at[0, x], n_s.at[i], n_r.at[i], zhi).wait_recv()
    for i in range(4):
        remote(n_own, n_all.at[1, x], n_s.at[4 + i], n_r.at[4 + i], zhi).wait_recv()
    for block in range(2):
        cosine, sine = angles(140 + 2 * y + (h if block == 0 else far), 48)
        for j in range(2):
            raw = n_all[block, 2 * j].astype(F32)
            spot = block * 48
            new_keys[j, spot : spot + 48, :] = turn(raw, cosine, sine).astype(BF16)
            new_vals[j, spot : spot + 48, :] = n_all[block, 2 * j + 1]
    pair.wait_recv()

    def turn_queries(b, carry):
        cosine, sine = angles(140 + 2 * b + h, 48)
        for head in range(8):
            raw = q_all[head % 2, b, head // 2].astype(F32)
            spot = (head % 4) * 48
            q_rot[head // 4, b, spot : spot + 48, :] = turn(raw, cosine, sine).astype(BF16)
        return carry

    lax.fori_loop(0, 4, turn_queries, 0)

    for i in range(3):
        came = kv_far.at[2 * up(x, 3 - i) + k]
        remote(came, came, kf_s.at[i], kf_r.at[i], twin).wait_recv()
        go(remote(came, came, kt_s.at[i], kt_r.at[i], twin))
    for i in range(4):
        came = kv_far.at[2 * up(x, 3 - i) + 1 - k]
        remote(came, came, kt_s.at[i], kt_r.at[i], twin).wait_recv()
    far_rows = kv_far[...].reshape(half, 2, 256)
    for page in range(6):
        place_page(1, page, far_rows[page * 128 : page * 128 + 128])

    scale = 128 ** (-0.5)
    lane = lax.broadcasted_iota(jnp.int32, (48, 128), 1)
    key_lane = lax.broadcasted_iota(jnp.int32, (192, 128), 1)
    token = lax.broadcasted_iota(jnp.int32, (4, 48, 128), 1).reshape(192, 128)
    first = (2 * y + h) * 48
    second = (2 * y + far) * 48
    key_index = jnp.where(
        key_lane < 48, first + key_lane, jnp.where(key_lane < 96, second + key_lane - 48, 1 << 20)
    )
    nt = (((1,), (1,)), ((), ()))

    def attend(step, carry):
        j = step // 4
        i = step % 4
        b = up(y, i + 1)
        query = q_rot[j, b]
        scores = lax.dot_general(query, keys[j], nt, preferred_element_type=F32)
        expo = jnp.where(live[0:1, :] > 0.5, jnp.exp(scores * scale), 0.0)
        recent = lax.dot_general(query, new_keys[j], nt, preferred_element_type=F32)
        seen = key_index <= (2 * b + h) * 48 + token
        recent_expo = jnp.where(seen, jnp.exp(recent * scale), 0.0)
        denom = jnp.sum(expo, axis=1, keepdims=True) + jnp.sum(recent_expo, axis=1, keepdims=True)
        numer = jnp.dot(expo.astype(BF16), vals[j], preferred_element_type=F32)
        numer = numer + jnp.dot(recent_expo.astype(BF16), new_vals[j], preferred_element_type=F32)
        lanes = jnp.zeros((48, 128), F32)
        for g in range(4):
            lanes = lanes + jnp.where(lane == j * 4 + g, denom[g * 48 : g * 48 + 48], 0.0)

        @pl.when(i < 3)
        def _():
            num_out[j, i] = numer.astype(BF16)
            remote(
                num_out.at[j, i], num_in.at[j, i], num_s.at[j, i], num_r.at[j, i], dev(x, k, b, h, m)
            ).start()

            @pl.when(j == 0)
            def _():
                den_out[i] = lanes

            @pl.when(j == 1)
            def _():
                den_out[i] = den_out[i] + lanes
                remote(
                    den_out.at[i], den_in.at[i], den_s.at[i], den_r.at[i], dev(x, k, b, h, m)
                ).start()

        @pl.when(i == 3)
        def _():
            num_own[j] = numer

            @pl.when(j == 0)
            def _():
                den_own[...] = lanes

            @pl.when(j == 1)
            def _():
                den_own[...] = den_own[...] + lanes

        return carry

    lax.fori_loop(0, 8, attend, 0)
    send_far(2)
    for p in range(4):
        near_ring.forward(p)
    for p in (0, 1):
        take_far(p)

    denom = den_own[...]
    for i in range(3):
        copy = remote(den_out.at[i], den_in.at[i], den_s.at[i], den_r.at[i], dev(x, k, up(y, i + 1), h, m))
        copy.wait()
        denom = denom + den_in[i]
    for j in range(2):
        numer = num_own[j]
        for i in range(3):
            remote(
                num_out.at[j, i],
                num_in.at[j, i],
                num_s.at[j, i],
                num_r.at[j, i],
                dev(x, k, up(y, i + 1), h, m),
            ).wait()
            numer = numer + num_in[j, i].astype(F32)
        for g in range(4):
            head = j * 4 + g
            attn_all[m, pl.ds(pl.multiple_of(x * 48, 16), 48), head * 128 : head * 128 + 128] = (
                numer[g * 48 : g * 48 + 48] / denom[:, head : head + 1]
            ).astype(BF16)


    def gather(view, zs, zr, xs, xr):
        own = view(x, m)
        for i, b in enumerate(m_peers):
            go(remote(own, own, zs.at[i], zr.at[i], at_m(b)))
        for j, a in enumerate(x_peers):
            go(remote(own, own, xs.at[3, j], xr.at[3, j], at_x(a)))
        for i in range(3):
            came = view(x, up(m, 3 - i))
            remote(own, came, zs.at[i], zr.at[i], at_m(m_peers[i])).wait_recv()
            for j, a in enumerate(x_peers):
                go(remote(came, came, xs.at[i, j], xr.at[i, j], at_x(a)))

    def gather_rest(view, xs, xr):
        for i in (3, 0, 1, 2):
            for j in range(3):
                came = view(up(x, 3 - j), up(m, 3 - i) if i < 3 else m)
                remote(came, came, xs.at[i, j], xr.at[i, j], at_x(x_peers[j])).wait_recv()

    def attn_view(a, b):
        return attn_all.at[b, pl.ds(pl.multiple_of(a * 48, 16), 48)]

    gather(attn_view, az_s, az_r, ax_s, ax_r)
    send_far(3)
    for p in range(4):
        near_ring.collect(p)
    take_far(2)
    for p in (0, 1):
        far_ring.forward(p)
    gather_rest(attn_view, ax_s, ax_r)
    local[0].wait()
    shared[0].wait_recv()

    total = jnp.dot(attn_all[0], out_w[0:1024, :], preferred_element_type=F32)
    for b in range(1, 4):
        total = total + jnp.dot(
            attn_all[b], out_w[b * 1024 : b * 1024 + 1024, :], preferred_element_type=F32
        )
    even = pl.ds(pl.multiple_of((8 * x + m) * 128, 128), 128)
    odd = pl.ds(pl.multiple_of((8 * x + 4 + m) * 128, 128), 128)
    columns = jnp.concatenate([states[:, even], states[:, odd]], axis=1).astype(F32)
    gains = jnp.concatenate([gain[:, even], gain[:, odd]], axis=1)
    kept = total + jnp.concatenate([columns] * 4, axis=0)
    resid[...] = kept

    def shard_view(a, b):
        return shards.at[a, b]

    shards[x, m] = (kept * gains).astype(BF16)
    gather(shard_view, gz_s, gz_r, gx_s, gx_r)

    take_far(3)
    far_ring.forward(2)
    gather_rest(shard_view, gx_s, gx_r)
    far_ring.forward(3)

    squares = jnp.zeros((192, 128), F32)
    for a in range(4):
        for b in range(4):
            for e in range(2):
                block = shards[a, b, :, e * 128 : e * 128 + 128]
                normed[2 * a + e, :, b * 128 : b * 128 + 128] = block
                spot = (8 * a + 4 * e + b) * 128
                plain = block.astype(F32) / gain[:, spot : spot + 128]
                squares = squares + plain * plain
    ratio = lax.rsqrt(jnp.sum(squares, axis=1, keepdims=True) / 4096 + EPSILON)

    for copy in local[1:]:
        copy.wait()
    for copy in shared[1:]:
        copy.wait_recv()
    near_ring.done()

    acc[...] = jnp.zeros(acc.shape, F32)

    def gate_up(step, carry):
        s = 2 * lax.rem(step, 4) + jnp.where(step < 4, h, far)
        for cc in range(2):
            for part in range(2):
                acc[cc, part] = acc[cc, part] + lax.dot_general(
                    normed[s],
                    gate_up_w[cc, s, part * 448 : part * 448 + 448, :],
                    nt,
                    preferred_element_type=F32,
                )
        return carry

    lax.fori_loop(0, 4, gate_up, 0)
    for p in range(4):
        far_ring.collect(p)
    for p in range(4):
        ref = gate_up_w.at[1 - k, far_s, pl.ds(p * 224, 224)]
        remote(ref, ref, core_s.at[3 + p], core_r.at[3 + p], twin).wait_recv()
    far_ring.done()
    lax.fori_loop(4, 8, gate_up, 0)
    for cc in range(2):
        gate = acc[cc, 0] * ratio
        upward = acc[cc, 1] * ratio
        inner[cc] = (gate / (1.0 + jnp.exp(-gate)) * upward).astype(BF16)

    def down(step, carry):
        zi = step // 4
        xi = step % 4
        b = up(m, zi + 1)
        a = up(x, xi + 1)
        first = pl.ds(pl.multiple_of((8 * a + b) * 128, 128), 128)
        second = pl.ds(pl.multiple_of((8 * a + 4 + b) * 128, 128), 128)
        block = jnp.zeros((192, 256), F32)
        for cc in range(2):
            weights = jnp.concatenate([down_w[cc, :, first], down_w[cc, :, second]], axis=1)
            block = block + jnp.dot(inner[cc], weights, preferred_element_type=F32)

        @pl.when(xi < 3)
        def _():
            x_out[xi, zi] = block.astype(BF16)
            remote(
                x_out.at[xi, zi], x_in.at[xi, zi], rx_s.at[xi, zi], rx_r.at[xi, zi], at_x(a)
            ).start()

        @pl.when(xi == 3)
        def _():
            x_own[zi] = block

        return carry

    lax.fori_loop(0, 16, down, 0)
    for zi in range(4):
        block = x_own[zi]
        for xi in range(3):
            remote(
                x_out.at[xi, zi], x_in.at[xi, zi], rx_s.at[xi, zi], rx_r.at[xi, zi], at_x(x_peers[xi])
            ).wait()
            block = block + x_in[xi, zi].astype(F32)
        if zi < 3:
            z_out[zi] = block.astype(BF16)
            go(remote(z_out.at[zi], z_in.at[zi], rz_s.at[zi], rz_r.at[zi], at_m(m_peers[zi])))
    block = block + resid[...]
    for zi in range(3):
        remote(z_out.at[zi], z_in.at[zi], rz_s.at[zi], rz_r.at[zi], at_m(m_peers[zi])).wait_recv()
        block = block + z_in[zi].astype(F32)
    result = block.astype(BF16)
    lower = result[:, :128]
    upper = result[:, 128:]
    swap_out[...] = jnp.where(k == 0, upper, lower)
    swap = go(remote(swap_out, swap_in, sw_s, sw_r, twin))
    kept_half = jnp.where(k == 0, lower, upper)
    for a in range(4):
        out[a, k] = kept_half[a * 48 : a * 48 + 48]
    swap.wait_recv()
    for a in range(4):
        out[a, 1 - k] = swap_in[a * 48 : a * 48 + 48, :]
    for copy in sends:
        copy.wait_send()


def per_device(
    states,
    attn_gain,
    w_query,
    w_keyval,
    kv_cache,
    page_live,
    factor_levels,
    cand_index,
    w_out,
    ffn_gain,
    w_gate_up,
    w_down,
):
    w_shard = jnp.swapaxes(w_gate_up, 1, 2).reshape(896, 512)

    vmem = pl.BlockSpec(memory_space=pltpu.VMEM)
    hbm = pl.BlockSpec(memory_space=pl.ANY)
    smem = pl.BlockSpec(memory_space=pltpu.SMEM)
    out = pl.pallas_call(
        layer_kernel,
        out_shape=jax.ShapeDtypeStruct((4, 2, 48, 128), BF16),
        in_specs=[smem] * 2 + [vmem] * 7 + [hbm] * 3,
        out_specs=vmem,
        scratch_shapes=[
            VM((8, 48, 256), BF16),
            VM((152, 128), F32),
            VM((152, 128), F32),
            VM((8, 128), F32),
            VM((7, 48, 256), BF16),
            VM((48, 128), BF16),
            VM((48, 128), BF16),
            VM((2, 4, 4, 48, 128), BF16),
            VM((2, 4, 48, 128), BF16),
            VM((8, 96, 2, 256), BF16),
            VM((8, 128), F32),
            VM((2, 1536, 128), BF16),
            VM((2, 1536, 128), BF16),
            VM((2, 128, 128), BF16),
            VM((2, 128, 128), BF16),
            VM((8, 1536), F32),
            VM((2, 4, 192, 128), BF16),
            VM((2, 3, 192, 128), BF16),
            VM((2, 3, 192, 128), BF16),
            VM((2, 192, 128), F32),
            VM((3, 48, 128), F32),
            VM((3, 48, 128), F32),
            VM((48, 128), F32),
            VM((4, 192, 1024), BF16),
            VM((4096, 256), BF16),
            VM((2, 8, 896, 512), BF16),
            VM((2, 448, 4096), BF16),
            VM((192, 256), F32),
            VM((4, 4, 192, 256), BF16),
            VM((8, 192, 512), BF16),
            VM((2, 2, 192, 448), F32),
            VM((2, 192, 448), BF16),
            VM((3, 4, 192, 256), BF16),
            VM((3, 4, 192, 256), BF16),
            VM((4, 192, 256), F32),
            VM((3, 192, 256), BF16),
            VM((3, 192, 256), BF16),
            VM((192, 128), BF16),
            VM((192, 128), BF16),
            DMA((7,)),
            DMA((7,)),
            DMA((15,)),
            DMA((15,)),
            DMA((8,)),
            DMA((8,)),
            DMA,
            DMA,
            DMA((3,)),
            DMA((3,)),
            DMA((4,)),
            DMA((4,)),
            DMA,
            DMA,
            DMA,
            DMA,
            DMA((2, 3)),
            DMA((2, 3)),
            DMA((3,)),
            DMA((3,)),
            DMA((4,)),
            DMA((4,)),
            DMA((2, 3, 4)),
            DMA((2, 3, 4)),
            DMA((2, 3, 4)),
            DMA((2, 3, 4)),
            DMA((7,)),
            DMA((7,)),
            DMA((3,)),
            DMA((3,)),
            DMA((4, 3)),
            DMA((4, 3)),
            DMA((3,)),
            DMA((3,)),
            DMA((4, 3)),
            DMA((4, 3)),
            DMA((3, 4)),
            DMA((3, 4)),
            DMA((3,)),
            DMA((3,)),
            DMA,
            DMA,
            DMA((3,)),
        ],
        compiler_params=pltpu.CompilerParams(
            collective_id=0, has_side_effects=True, vmem_limit_bytes=60 << 20
        ),
        name="layer",
    )(
        page_live,
        factor_levels,
        cand_index,
        attn_gain.reshape(1, 4096),
        w_query,
        w_keyval,
        kv_cache,
        states,
        ffn_gain.reshape(1, 4096),
        w_shard,
        w_out,
        w_down,
    )
    return out.reshape(8, 48, 128)


def solution(mesh):
    return jax.shard_map(
        per_device,
        mesh=mesh,
        in_specs=(
            P("ctx", None),
            P(),
            P("cand", "mp", None),
            P("cand", "mp", None),
            P("ctx", "mp", None),
            P("ctx"),
            P(),
            P("cand", None),
            P(None, ("cand", "mp")),
            P(),
            P(None, "ctx", ("cand", "mp")),
            P(("cand", "mp"), None),
        ),
        out_specs=P(None, "ctx", ("cand", "mp")),
        check_vma=False,
    )
```

```python
import functools
import math

import jax
import jax.numpy as jnp
from jax import lax
from jax.experimental import pallas as pl
from jax.experimental.pallas import tpu as pltpu
from jax.sharding import PartitionSpec as P

EPSILON = 1e-05
ROPE_BASE = 500000.0
MESH = pl.DeviceIdType.MESH
F32 = jnp.float32
BF16 = jnp.bfloat16
DMA = pltpu.SemaphoreType.DMA
VM = pltpu.VMEM


def position():
    c = lax.axis_index("cand")
    s = lax.axis_index("ctx")
    m = lax.axis_index("mp")
    return c // 2, c % 2, s // 2, s % 2, m


def dev(x, k, y, h, m):
    return {"cand": x * 2 + k, "ctx": y * 2 + h, "mp": m}


def up(value, step, size=4):
    return lax.rem(value + step, size)


def remote(src, dst, send_sem, recv_sem, target):
    return pltpu.make_async_remote_copy(
        src_ref=src,
        dst_ref=dst,
        send_sem=send_sem,
        recv_sem=recv_sem,
        device_id=target,
        device_id_type=MESH,
    )


def greet(peers, work):
    barrier = pltpu.get_barrier_semaphore()
    for peer in peers:
        pl.semaphore_signal(barrier, inc=1, device_id=peer, device_id_type=MESH)
    work()
    pl.semaphore_wait(barrier, len(peers))


def turn(values, cosine, sine):
    return values * cosine + pltpu.roll(values, 64, 1) * sine


class Ring:
    def __init__(self, go, me, at, twin, view, send_sem, recv_sem, twin_send, twin_recv):
        self.go, self.me, self.at, self.twin, self.view = go, me, at, twin, view
        self.ss, self.rs, self.ts, self.tr = send_sem, recv_sem, twin_send, twin_recv

    def copy(self, src, dst, kind, part, step):
        return remote(src, dst, self.ss.at[kind, part], self.rs.at[kind, part], self.at(up(self.me, step)))

    def send(self, part, src):
        dst = self.view(self.me, part)
        steps = (1, 3) if part % 2 == 0 else (3, 1)
        for step in steps:
            self.go(self.copy(src, dst, 0 if step == 1 else 1, part, step))

    def take(self, kind, part):
        ref = self.view(up(self.me, (3, 1, 2)[kind]), part)
        self.copy(ref, ref, kind, part, 1).wait_recv()
        self.go(remote(ref, ref, self.ts.at[kind, part], self.tr.at[kind, part], self.twin))
        return ref

    def forward(self, part):
        ref = self.take(part % 2, part)
        self.go(self.copy(ref, ref, 2, part, 1 if part % 2 == 0 else 3))

    def collect(self, part):
        self.take(1 - part % 2, part)
        self.take(2, part)

    def done(self):
        for kind in range(3):
            for part in range(4):
                ref = self.view(up(self.me, (3, 1, 2)[kind]), part)
                remote(ref, ref, self.ts.at[kind, part], self.tr.at[kind, part], self.twin).wait_recv()


def layer_kernel(
    live_pages,
    levels,
    picks,
    attn_gain,
    w_query,
    w_keyval,
    kv,
    states,
    gain,
    w_shard,
    w_out,
    w_down,
    out,
    part,
    cosines,
    sines,
    flags,
    rs_in,
    q_own,
    n_own,
    q_all,
    n_all,
    kv_far,
    flags_far,
    keys,
    vals,
    new_keys,
    new_vals,
    live,
    q_rot,
    num_out,
    num_in,
    num_own,
    den_out,
    den_in,
    den_own,
    attn_all,
    out_w,
    gate_up_w,
    down_w,
    resid,
    shards,
    normed,
    acc,
    inner,
    x_out,
    x_in,
    x_own,
    z_out,
    z_in,
    swap_out,
    swap_in,
    rs_s,
    rs_r,
    q_s,
    q_r,
    n_s,
    n_r,
    kz_s,
    kz_r,
    kf_s,
    kf_r,
    kt_s,
    kt_r,
    qt_s,
    qt_r,
    fl_s,
    fl_r,
    num_s,
    num_r,
    den_s,
    den_r,
    wz_s,
    wz_r,
    ring_s,
    ring_r,
    tw_s,
    tw_r,
    core_s,
    core_r,
    az_s,
    az_r,
    ax_s,
    ax_r,
    gz_s,
    gz_r,
    gx_s,
    gx_r,
    rx_s,
    rx_r,
    rz_s,
    rz_r,
    sw_s,
    sw_r,
    loc,
):
    x, k, y, h, m = position()
    c = x * 2 + k
    far = 1 - h
    cand_peers = [(x, 1 - k)] + [(up(x, i), kk) for i in (1, 2, 3) for kk in (k, 1 - k)]
    xy_peers = [(up(x, i), up(y, j)) for j in range(4) for i in range(4) if i or j]
    zhi = dev(x, k, y, far, m)
    x_peers = [up(x, i) for i in (1, 2, 3)]
    m_peers = [up(m, i) for i in (1, 2, 3)]
    twin = dev(x, 1 - k, y, h, m)
    near_s = 2 * y + h
    far_s = 2 * y + far

    def at_x(a):
        return dev(a, k, y, h, m)

    def at_y(a):
        return dev(x, k, a, h, m)

    def at_m(a):
        return dev(x, k, y, h, a)

    def prepare():
        values = states[...].astype(F32)
        ratio = lax.rsqrt(jnp.sum(values * values, axis=1, keepdims=True) / 4096 + EPSILON)
        slab = pl.ds(pl.multiple_of(c * 512, 512), 512)
        normed_slab = (states[:, slab].astype(F32) * ratio * attn_gain[:, slab]).astype(BF16)
        for j in range(2):
            queries = jnp.dot(normed_slab, w_query[:, j, :], preferred_element_type=F32).astype(BF16)
            keyvals = jnp.dot(normed_slab, w_keyval[:, j, :], preferred_element_type=F32).astype(BF16)
            for g in range(4):
                part[4 * j + g, :, :128] = queries[:, g * 128 : g * 128 + 128]
                spot = g // 2 * 128
                part[4 * j + g, :, 128:] = keyvals[:, spot : spot + 128]

    def mark_pages():
        page_lane = lax.broadcasted_iota(jnp.int32, (8, 128), 1)
        marks = jnp.zeros((8, 128), F32)
        for page in range(6):
            marks = jnp.where(page_lane == page, live_pages[page].astype(F32), marks)
        flags[...] = marks

    def make_tables():
        pick = jnp.concatenate([picks[...], picks[...]], axis=1)
        factor = jnp.zeros((1, 128), F32)
        for level in range(16):
            factor = jnp.where(pick == level, levels[level], factor)
        lane = lax.broadcasted_iota(jnp.int32, (1, 128), 1)
        step = jnp.where(lane < 64, lane, lane - 64).astype(F32)
        freq = jnp.exp(step * (-2.0 * math.log(ROPE_BASE) / 128)) / factor
        row = lax.broadcasted_iota(jnp.int32, (152, 128), 0)
        near = near_s * 768 + 128 * (row - 128)
        other = far_s * 768 + 128 * (row - 134)
        where = jnp.where(
            row < 128, row, jnp.where(row < 134, near, jnp.where(row < 140, other, 6144 + 48 * (row - 140)))
        )
        angle = where.astype(F32) * freq
        cosines[...] = jnp.cos(angle)
        sines[...] = jnp.sin(angle)

    greet(
        [dev(a, b, y, h, m) for a, b in cand_peers]
        + [dev(a, k, b, h, m) for a, b in xy_peers[3:]]
        + [dev(up(x, i), k, y, far, m) for i in range(4)]
        + [at_m(a) for a in m_peers],
        lambda: (mark_pages(), prepare()),
    )
    rows = kv_far.shape[1]
    sends = []

    def go(copy):
        copy.start()
        sends.append(copy)
        return copy

    mine = kv.at[pl.ds(pl.multiple_of(c * rows, 16), rows)]
    kz = go(remote(mine, kv_far.at[c], kz_s, kz_r, zhi))
    fl = go(remote(flags, flags_far, fl_s, fl_r, zhi))
    side = pl.ds(pl.multiple_of(k * 128, 128), 128)
    pairs = [
        (w_out, out_w.at[:, side]),
        (w_shard, gate_up_w.at[k, near_s]),
        (w_down, down_w.at[k]),
    ]
    local = []
    shared = []
    for i, (src, dst) in enumerate(pairs):
        copy = pltpu.make_async_copy(src, dst, loc.at[i])
        copy.start()
        local.append(copy)
        shared.append(go(remote(src, dst, core_s.at[i], core_r.at[i], twin)))

    def near_view(b, part):
        return gate_up_w.at[k, 2 * b + h, pl.ds(part * 224, 224)]

    def far_view(b, part):
        return gate_up_w.at[k, 2 * b + far, pl.ds(part * 224, 224)]

    near_ring = Ring(go, y, at_y, twin, near_view, ring_s.at[0], ring_r.at[0], tw_s.at[0], tw_r.at[0])
    far_ring = Ring(go, y, at_y, twin, far_view, ring_s.at[1], ring_r.at[1], tw_s.at[1], tw_r.at[1])

    def send_near(p):
        near_ring.send(p, w_shard.at[pl.ds(p * 224, 224)])

    def send_far(p):
        go(remote(w_shard.at[pl.ds(p * 224, 224)], near_view(y, p), wz_s.at[p], wz_r.at[p], zhi))

    def take_far(p):
        ref = far_view(y, p)
        remote(ref, ref, wz_s.at[p], wz_r.at[p], zhi).wait_recv()
        go(remote(ref, ref, core_s.at[3 + p], core_r.at[3 + p], twin))
        far_ring.send(p, ref)

    for p in (0,):
        send_near(p)
    send_near(1)
    for i, (a, b) in enumerate(cand_peers):
        go(remote(part.at[2 * a + b], rs_in.at[i], rs_s.at[i], rs_r.at[i], dev(a, b, y, h, m)))
    half = kv.shape[0]

    make_tables()
    sign = jnp.where(lax.broadcasted_iota(jnp.int32, (1, 128), 1) < 64, -1.0, 1.0)

    def angles(base, count):
        first_cos = cosines[pl.ds(base, 1), :]
        first_sin = sines[pl.ds(base, 1), :]
        place_cos = cosines[pl.ds(0, count), :]
        place_sin = sines[pl.ds(0, count), :]
        return (
            first_cos * place_cos - first_sin * place_sin,
            (first_sin * place_cos + first_cos * place_sin) * sign,
        )

    def place_page(side, page, source):
        cosine, sine = angles(128 + side * 6 + page, 128)
        rows = pl.ds(side * half + page * 128, 128)
        for j in range(2):
            raw = source[:, j, :128].astype(F32)
            keys[j, rows, :] = turn(raw, cosine, sine).astype(BF16)
            vals[j, rows, :] = source[:, j, 128:]

    for page in range(6):
        place_page(0, page, kv[page * 128 : page * 128 + 128])
    for j in range(2):
        new_keys[j] = jnp.zeros(new_keys.shape[1:], BF16)
        new_vals[j] = jnp.zeros(new_vals.shape[1:], BF16)

    for i, (a, b) in enumerate(cand_peers):
        remote(part.at[c], rs_in.at[i], rs_s.at[i], rs_r.at[i], dev(a, b, y, h, m)).wait_recv()
    total = part[c].astype(F32)
    for i in range(7):
        total = total + rs_in[i].astype(F32)
    summed = total.astype(BF16)
    q_own[...] = summed[:, :128]
    n_own[...] = summed[:, 128:]
    q_all[k, y, x] = summed[:, :128]
    n_all[0, x] = summed[:, 128:]
    for i, (a, b) in enumerate(xy_peers):
        go(remote(q_own, q_all.at[k, y, x], q_s.at[i], q_r.at[i], dev(a, k, b, h, m)))
    for i in (1, 2, 3):
        go(remote(n_own, n_all.at[0, x], n_s.at[i], n_r.at[i], dev(up(x, i), k, y, h, m)))
    for i in range(4):
        go(remote(n_own, n_all.at[1, x], n_s.at[4 + i], n_r.at[4 + i], dev(up(x, i), k, y, far, m)))

    for p in (0, 1):
        send_far(p)
    for p in (2, 3):
        send_near(p)
    kz.wait_recv()
    for i, a in enumerate(x_peers):
        go(remote(kv_far.at[c], kv_far.at[c], kf_s.at[i], kf_r.at[i], at_x(a)))
    go(remote(kv_far.at[c], kv_far.at[c], kt_s.at[3], kt_r.at[3], twin))
    fl.wait_recv()
    for page in range(6):
        live[:, page * 128 : page * 128 + 128] = jnp.broadcast_to(flags[:, page : page + 1], (8, 128))
        live[:, half + page * 128 : half + page * 128 + 128] = jnp.broadcast_to(
            flags_far[:, page : page + 1], (8, 128)
        )

    for i, (a, b) in enumerate(xy_peers):
        remote(q_own, q_all.at[k, b, a], q_s.at[i], q_r.at[i], dev(a, k, b, h, m)).wait_recv()
    pair = go(remote(q_all.at[k], q_all.at[k], qt_s, qt_r, twin))
    for i in (1, 2, 3):
        remote(n_own, n_all.at[0, x], n_s.at[i], n_r.at[i], zhi).wait_recv()
    for i in range(4):
        remote(n_own, n_all.at[1, x], n_s.at[4 + i], n_r.at[4 + i], zhi).wait_recv()
    for block in range(2):
        cosine, sine = angles(140 + 2 * y + (h if block == 0 else far), 48)
        for j in range(2):
            raw = n_all[block, 2 * j].astype(F32)
            spot = block * 48
            new_keys[j, spot : spot + 48, :] = turn(raw, cosine, sine).astype(BF16)
            new_vals[j, spot : spot + 48, :] = n_all[block, 2 * j + 1]
    pair.wait_recv()

    def turn_queries(b, carry):
        cosine, sine = angles(140 + 2 * b + h, 48)
        for head in range(8):
            raw = q_all[head % 2, b, head // 2].astype(F32)
            spot = (head % 4) * 48
            q_rot[head // 4, b, spot : spot + 48, :] = turn(raw, cosine, sine).astype(BF16)
        return carry

    lax.fori_loop(0, 4, turn_queries, 0)

    for i in range(3):
        came = kv_far.at[2 * up(x, 3 - i) + k]
        remote(came, came, kf_s.at[i], kf_r.at[i], twin).wait_recv()
        go(remote(came, came, kt_s.at[i], kt_r.at[i], twin))
    for i in range(4):
        came = kv_far.at[2 * up(x, 3 - i) + 1 - k]
        remote(came, came, kt_s.at[i], kt_r.at[i], twin).wait_recv()
    far_rows = kv_far[...].reshape(half, 2, 256)
    for page in range(6):
        place_page(1, page, far_rows[page * 128 : page * 128 + 128])

    scale = 128 ** (-0.5)
    lane = lax.broadcasted_iota(jnp.int32, (48, 128), 1)
    key_lane = lax.broadcasted_iota(jnp.int32, (192, 128), 1)
    token = lax.broadcasted_iota(jnp.int32, (4, 48, 128), 1).reshape(192, 128)
    first = (2 * y + h) * 48
    second = (2 * y + far) * 48
    key_index = jnp.where(
        key_lane < 48, first + key_lane, jnp.where(key_lane < 96, second + key_lane - 48, 1 << 20)
    )
    nt = (((1,), (1,)), ((), ()))

    def attend(step, carry):
        j = step // 4
        i = step % 4
        b = up(y, i + 1)
        query = q_rot[j, b]
        scores = lax.dot_general(query, keys[j], nt, preferred_element_type=F32)
        expo = jnp.where(live[0:1, :] > 0.5, jnp.exp(scores * scale), 0.0)
        recent = lax.dot_general(query, new_keys[j], nt, preferred_element_type=F32)
        seen = key_index <= (2 * b + h) * 48 + token
        recent_expo = jnp.where(seen, jnp.exp(recent * scale), 0.0)
        denom = jnp.sum(expo, axis=1, keepdims=True) + jnp.sum(recent_expo, axis=1, keepdims=True)
        numer = jnp.dot(expo.astype(BF16), vals[j], preferred_element_type=F32)
        numer = numer + jnp.dot(recent_expo.astype(BF16), new_vals[j], preferred_element_type=F32)
        lanes = jnp.zeros((48, 128), F32)
        for g in range(4):
            lanes = lanes + jnp.where(lane == j * 4 + g, denom[g * 48 : g * 48 + 48], 0.0)

        @pl.when(i < 3)
        def _():
            num_out[j, i] = numer.astype(BF16)
            remote(
                num_out.at[j, i], num_in.at[j, i], num_s.at[j, i], num_r.at[j, i], dev(x, k, b, h, m)
            ).start()

            @pl.when(j == 0)
            def _():
                den_out[i] = lanes

            @pl.when(j == 1)
            def _():
                den_out[i] = den_out[i] + lanes
                remote(
                    den_out.at[i], den_in.at[i], den_s.at[i], den_r.at[i], dev(x, k, b, h, m)
                ).start()

        @pl.when(i == 3)
        def _():
            num_own[j] = numer

            @pl.when(j == 0)
            def _():
                den_own[...] = lanes

            @pl.when(j == 1)
            def _():
                den_own[...] = den_own[...] + lanes

        return carry

    lax.fori_loop(0, 8, attend, 0)
    send_far(2)
    for p in range(4):
        near_ring.forward(p)
    for p in (0, 1):
        take_far(p)

    denom = den_own[...]
    for i in range(3):
        copy = remote(den_out.at[i], den_in.at[i], den_s.at[i], den_r.at[i], dev(x, k, up(y, i + 1), h, m))
        copy.wait()
        denom = denom + den_in[i]
    for j in range(2):
        numer = num_own[j]
        for i in range(3):
            remote(
                num_out.at[j, i],
                num_in.at[j, i],
                num_s.at[j, i],
                num_r.at[j, i],
                dev(x, k, up(y, i + 1), h, m),
            ).wait()
            numer = numer + num_in[j, i].astype(F32)
        for g in range(4):
            head = j * 4 + g
            attn_all[m, pl.ds(pl.multiple_of(x * 48, 16), 48), head * 128 : head * 128 + 128] = (
                numer[g * 48 : g * 48 + 48] / denom[:, head : head + 1]
            ).astype(BF16)


    def gather(view, zs, zr, xs, xr):
        own = view(x, m)
        for i, b in enumerate(m_peers):
            go(remote(own, own, zs.at[i], zr.at[i], at_m(b)))
        for j, a in enumerate(x_peers):
            go(remote(own, own, xs.at[3, j], xr.at[3, j], at_x(a)))
        for i in range(3):
            came = view(x, up(m, 3 - i))
            remote(own, came, zs.at[i], zr.at[i], at_m(m_peers[i])).wait_recv()
            for j, a in enumerate(x_peers):
                go(remote(came, came, xs.at[i, j], xr.at[i, j], at_x(a)))

    def gather_rest(view, xs, xr):
        for i in (3, 0, 1, 2):
            for j in range(3):
                came = view(up(x, 3 - j), up(m, 3 - i) if i < 3 else m)
                remote(came, came, xs.at[i, j], xr.at[i, j], at_x(x_peers[j])).wait_recv()

    def attn_view(a, b):
        return attn_all.at[b, pl.ds(pl.multiple_of(a * 48, 16), 48)]

    gather(attn_view, az_s, az_r, ax_s, ax_r)
    send_far(3)
    for p in range(4):
        near_ring.collect(p)
    take_far(2)
    for p in (0, 1):
        far_ring.forward(p)
    gather_rest(attn_view, ax_s, ax_r)
    local[0].wait()
    shared[0].wait_recv()

    total = jnp.dot(attn_all[0], out_w[0:1024, :], preferred_element_type=F32)
    for b in range(1, 4):
        total = total + jnp.dot(
            attn_all[b], out_w[b * 1024 : b * 1024 + 1024, :], preferred_element_type=F32
        )
    even = pl.ds(pl.multiple_of((8 * x + m) * 128, 128), 128)
    odd = pl.ds(pl.multiple_of((8 * x + 4 + m) * 128, 128), 128)
    columns = jnp.concatenate([states[:, even], states[:, odd]], axis=1).astype(F32)
    gains = jnp.concatenate([gain[:, even], gain[:, odd]], axis=1)
    kept = total + jnp.concatenate([columns] * 4, axis=0)
    resid[...] = kept

    def shard_view(a, b):
        return shards.at[a, b]

    shards[x, m] = (kept * gains).astype(BF16)
    gather(shard_view, gz_s, gz_r, gx_s, gx_r)

    take_far(3)
    far_ring.forward(2)
    gather_rest(shard_view, gx_s, gx_r)
    far_ring.forward(3)

    squares = jnp.zeros((192, 128), F32)
    for a in range(4):
        for b in range(4):
            for e in range(2):
                block = shards[a, b, :, e * 128 : e * 128 + 128]
                normed[2 * a + e, :, b * 128 : b * 128 + 128] = block
                spot = (8 * a + 4 * e + b) * 128
                plain = block.astype(F32) / gain[:, spot : spot + 128]
                squares = squares + plain * plain
    ratio = lax.rsqrt(jnp.sum(squares, axis=1, keepdims=True) / 4096 + EPSILON)

    for copy in local[1:]:
        copy.wait()
    for copy in shared[1:]:
        copy.wait_recv()
    near_ring.done()

    acc[...] = jnp.zeros(acc.shape, F32)

    def gate_up(step, carry):
        s = 2 * lax.rem(step, 4) + jnp.where(step < 4, h, far)
        for cc in range(2):
            for part in range(2):
                acc[cc, part] = acc[cc, part] + lax.dot_general(
                    normed[s],
                    gate_up_w[cc, s, part * 448 : part * 448 + 448, :],
                    nt,
                    preferred_element_type=F32,
                )
        return carry

    lax.fori_loop(0, 4, gate_up, 0)
    for p in range(4):
        far_ring.collect(p)
    for p in range(4):
        ref = gate_up_w.at[1 - k, far_s, pl.ds(p * 224, 224)]
        remote(ref, ref, core_s.at[3 + p], core_r.at[3 + p], twin).wait_recv()
    far_ring.done()
    lax.fori_loop(4, 8, gate_up, 0)
    for cc in range(2):
        gate = acc[cc, 0] * ratio
        upward = acc[cc, 1] * ratio
        inner[cc] = (gate / (1.0 + jnp.exp(-gate)) * upward).astype(BF16)

    def down(step, carry):
        zi = step // 4
        xi = step % 4
        b = up(m, zi + 1)
        a = up(x, xi + 1)
        first = pl.ds(pl.multiple_of((8 * a + b) * 128, 128), 128)
        second = pl.ds(pl.multiple_of((8 * a + 4 + b) * 128, 128), 128)
        block = jnp.zeros((192, 256), F32)
        for cc in range(2):
            weights = jnp.concatenate([down_w[cc, :, first], down_w[cc, :, second]], axis=1)
            block = block + jnp.dot(inner[cc], weights, preferred_element_type=F32)

        @pl.when(xi < 3)
        def _():
            x_out[xi, zi] = block.astype(BF16)
            remote(
                x_out.at[xi, zi], x_in.at[xi, zi], rx_s.at[xi, zi], rx_r.at[xi, zi], at_x(a)
            ).start()

        @pl.when(xi == 3)
        def _():
            x_own[zi] = block

        return carry

    lax.fori_loop(0, 16, down, 0)
    for zi in range(4):
        block = x_own[zi]
        for xi in range(3):
            remote(
                x_out.at[xi, zi], x_in.at[xi, zi], rx_s.at[xi, zi], rx_r.at[xi, zi], at_x(x_peers[xi])
            ).wait()
            block = block + x_in[xi, zi].astype(F32)
        if zi < 3:
            z_out[zi] = block.astype(BF16)
            go(remote(z_out.at[zi], z_in.at[zi], rz_s.at[zi], rz_r.at[zi], at_m(m_peers[zi])))
    block = block + resid[...]
    for zi in range(3):
        remote(z_out.at[zi], z_in.at[zi], rz_s.at[zi], rz_r.at[zi], at_m(m_peers[zi])).wait_recv()
        block = block + z_in[zi].astype(F32)
    result = block.astype(BF16)
    lower = result[:, :128]
    upper = result[:, 128:]
    swap_out[...] = jnp.where(k == 0, upper, lower)
    swap = go(remote(swap_out, swap_in, sw_s, sw_r, twin))
    kept_half = jnp.where(k == 0, lower, upper)
    for a in range(4):
        out[a, k] = kept_half[a * 48 : a * 48 + 48]
    swap.wait_recv()
    for a in range(4):
        out[a, 1 - k] = swap_in[a * 48 : a * 48 + 48, :]
    for copy in sends:
        copy.wait_send()


def per_device(
    states,
    attn_gain,
    w_query,
    w_keyval,
    kv_cache,
    page_live,
    factor_levels,
    cand_index,
    w_out,
    ffn_gain,
    w_gate_up,
    w_down,
):
    w_shard = jnp.swapaxes(w_gate_up, 1, 2).reshape(896, 512)

    vmem = pl.BlockSpec(memory_space=pltpu.VMEM)
    hbm = pl.BlockSpec(memory_space=pl.ANY)
    smem = pl.BlockSpec(memory_space=pltpu.SMEM)
    out = pl.pallas_call(
        layer_kernel,
        out_shape=jax.ShapeDtypeStruct((4, 2, 48, 128), BF16),
        in_specs=[smem] * 2 + [vmem] * 7 + [hbm] * 3,
        out_specs=vmem,
        scratch_shapes=[
            VM((8, 48, 256), BF16),
            VM((152, 128), F32),
            VM((152, 128), F32),
            VM((8, 128), F32),
            VM((7, 48, 256), BF16),
            VM((48, 128), BF16),
            VM((48, 128), BF16),
            VM((2, 4, 4, 48, 128), BF16),
            VM((2, 4, 48, 128), BF16),
            VM((8, 96, 2, 256), BF16),
            VM((8, 128), F32),
            VM((2, 1536, 128), BF16),
            VM((2, 1536, 128), BF16),
            VM((2, 128, 128), BF16),
            VM((2, 128, 128), BF16),
            VM((8, 1536), F32),
            VM((2, 4, 192, 128), BF16),
            VM((2, 3, 192, 128), BF16),
            VM((2, 3, 192, 128), BF16),
            VM((2, 192, 128), F32),
            VM((3, 48, 128), F32),
            VM((3, 48, 128), F32),
            VM((48, 128), F32),
            VM((4, 192, 1024), BF16),
            VM((4096, 256), BF16),
            VM((2, 8, 896, 512), BF16),
            VM((2, 448, 4096), BF16),
            VM((192, 256), F32),
            VM((4, 4, 192, 256), BF16),
            VM((8, 192, 512), BF16),
            VM((2, 2, 192, 448), F32),
            VM((2, 192, 448), BF16),
            VM((3, 4, 192, 256), BF16),
            VM((3, 4, 192, 256), BF16),
            VM((4, 192, 256), F32),
            VM((3, 192, 256), BF16),
            VM((3, 192, 256), BF16),
            VM((192, 128), BF16),
            VM((192, 128), BF16),
            DMA((7,)),
            DMA((7,)),
            DMA((15,)),
            DMA((15,)),
            DMA((8,)),
            DMA((8,)),
            DMA,
            DMA,
            DMA((3,)),
            DMA((3,)),
            DMA((4,)),
            DMA((4,)),
            DMA,
            DMA,
            DMA,
            DMA,
            DMA((2, 3)),
            DMA((2, 3)),
            DMA((3,)),
            DMA((3,)),
            DMA((4,)),
            DMA((4,)),
            DMA((2, 3, 4)),
            DMA((2, 3, 4)),
            DMA((2, 3, 4)),
            DMA((2, 3, 4)),
            DMA((7,)),
            DMA((7,)),
            DMA((3,)),
            DMA((3,)),
            DMA((4, 3)),
            DMA((4, 3)),
            DMA((3,)),
            DMA((3,)),
            DMA((4, 3)),
            DMA((4, 3)),
            DMA((3, 4)),
            DMA((3, 4)),
            DMA((3,)),
            DMA((3,)),
            DMA,
            DMA,
            DMA((3,)),
        ],
        compiler_params=pltpu.CompilerParams(
            collective_id=0, has_side_effects=True, vmem_limit_bytes=60 << 20
        ),
        name="layer",
    )(
        page_live,
        factor_levels,
        cand_index,
        attn_gain.reshape(1, 4096),
        w_query,
        w_keyval,
        kv_cache,
        states,
        ffn_gain.reshape(1, 4096),
        w_shard,
        w_out,
        w_down,
    )
    return out.reshape(8, 48, 128)


def solution(mesh):
    return jax.shard_map(
        per_device,
        mesh=mesh,
        in_specs=(
            P("ctx", None),
            P(),
            P("cand", "mp", None),
            P("cand", "mp", None),
            P("ctx", "mp", None),
            P("ctx"),
            P(),
            P("cand", None),
            P(None, ("cand", "mp")),
            P(),
            P(None, "ctx", ("cand", "mp")),
            P(("cand", "mp"), None),
        ),
        out_specs=P(None, "ctx", ("cand", "mp")),
        check_vma=False,
    )
```
